512 devices in a mesh: batch: 16 (over z), proto: 32 (over y, x, core).
Axes of the slice: x: 4, y: 4, z: 16, core: 2. Of those that a mesh axis runs over, the one named last changes fastest.
Arguments:
- embeddings: float32 [4096, 128], P(('batch', 'proto')), may hold values from -6 to 6
- prototypes: float32 [131072, 128], P(('batch', 'proto')), may hold values from -6 to 6
- partner: int32 [4096], P('batch'), may hold values from 0 to 4095, each once
Outputs:
- grad_embeddings: float32 [4096, 128], P(('batch', 'proto'))
- grad_prototypes: float32 [131072, 128], P(('batch', 'proto'))
The draws below stay inside these ranges and needn't reach their ends.
Inputs may be any that keep to these rules, and one draw needn't show every extreme that they name: partner is a permutation of the 4096 clips.
All inputs are finite; a program needn't handle non-finite values.
Results may differ from the reference program's by a relative error of at most 0.0003.
Values sent between devices are 32-bit elements; how exact they have to be, the bound alone decides.
No kernel may reach another device: no remote copies, remote signals or barrier semaphores. Data moves between devices by JAX's collectives and lax.ppermute only.
A program may use at most 64 MiB of HBM per device.

```python
import jax
import jax.numpy as jnp
from jax import lax

D = 128
PROTO_DEV = 4096
ITERS = 3
CLIPS = 4096
PROTOS = 131072
N_PROTO = 32


def level_of(rng, extent, shards, least, high):
    factor_of, own = 1.0, jax.random.fold_in(rng, 6)
    for dim, blocks in shards:
        heights = jnp.exp(jax.random.uniform(jax.random.fold_in(own, dim), (blocks,), jnp.float32, least / len(shards), high / len(shards)))
        factor_of = factor_of * jnp.repeat(heights, extent[dim] // blocks).reshape([-1 if axis == dim else 1 for axis in range(len(extent))])
    return factor_of


def gaussian(own_key, dims, width, reach, shards=(), held_as=jnp.bfloat16):
    values = width * jax.random.normal(own_key, dims, jnp.float32)
    if shards:
        values = values * level_of(own_key, dims, shards, -0.22, 0.18)
    return jnp.clip(values, -reach, reach).astype(held_as)


def setup_inputs(seed: int = 0) -> dict:
    seeds = jax.random.split(jax.random.key(seed), 4)
    embeddings = gaussian(seeds[0], (CLIPS, D), 1.0, 6.0, ((0, 512),), jnp.float32)
    prototypes = gaussian(seeds[1], (PROTOS, D), 1.0, 6.0, ((0, 512),), jnp.float32)
    partner = jax.random.permutation(seeds[2], CLIPS).astype(jnp.int32)
    return dict(embeddings=embeddings, prototypes=prototypes, partner=partner)


SINK_EPS = 0.05
SOFTMAX_TEMP = 0.1

def unit_rows(values):
    inverse = 1.0 / jnp.sqrt(lax.optimization_barrier(jnp.sum(values * values, axis=1, keepdims=True)) + 1e-06)
    return (values * inverse, inverse)

def pairwise_scores(left, right):
    return lax.dot_general(left, right, (((1,), (1,)), ((), ())), precision=lax.Precision.HIGHEST, preferred_element_type=jnp.float32)

def reference(embeddings, prototypes, partner):
    normalized_clips, clip_inverse = unit_rows(embeddings)
    unit_protos, proto_inverse = unit_rows(prototypes)
    blocks = unit_protos.reshape(N_PROTO, PROTO_DEV, D)
    row_scale = jnp.ones((CLIPS,), jnp.float32)
    softmax_denominator = jnp.zeros((CLIPS,), jnp.float32)
    col_scales = jnp.zeros((N_PROTO, PROTO_DEV), jnp.float32)
    for sweep in range(ITERS):

        def col_pass(carried, prototype_rows, scale_now=row_scale):
            running, softmax_accumulated = carried
            logit_scores = pairwise_scores(normalized_clips, prototype_rows)
            kernel = jnp.exp(logit_scores / SINK_EPS)
            col_scale = 1.0 / (PROTOS * lax.optimization_barrier(jnp.sum(kernel * scale_now[:, None], axis=0)))
            softmax_accumulated = softmax_accumulated + lax.optimization_barrier(jnp.sum(jnp.exp(logit_scores / SOFTMAX_TEMP), axis=1))
            return ((running + lax.optimization_barrier(jnp.sum(kernel * col_scale[None, :], axis=1)), softmax_accumulated), col_scale)
        (row_mass, soft_sum), col_scales = lax.scan(col_pass, (jnp.zeros((CLIPS,), jnp.float32), jnp.zeros((CLIPS,), jnp.float32)), blocks)
        if sweep == 0:
            softmax_denominator = soft_sum
        row_scale = 1.0 / (CLIPS * row_mass)
    mate_units = jnp.take(normalized_clips, partner, axis=0)
    mate_scale = jnp.take(row_scale, partner, axis=0)

    def grad_pass(running, element):
        prototype_rows, col_scale = element
        softmax_exponent = jnp.exp(pairwise_scores(normalized_clips, prototype_rows) / SOFTMAX_TEMP)
        assigned_target = CLIPS * jnp.exp(pairwise_scores(mate_units, prototype_rows) / SINK_EPS) * mate_scale[:, None] * col_scale[None, :]
        gradient_patch = (softmax_exponent / softmax_denominator[:, None] - assigned_target) / SOFTMAX_TEMP
        clip_part = jnp.dot(gradient_patch, prototype_rows, precision=lax.Precision.HIGHEST, preferred_element_type=jnp.float32)
        proto_part = lax.dot_general(gradient_patch, normalized_clips, (((0,), (0,)), ((), ())), precision=lax.Precision.HIGHEST, preferred_element_type=jnp.float32)
        return (running + clip_part, proto_part)
    clip_grads, proto_parts = lax.scan(grad_pass, jnp.zeros((CLIPS, D), jnp.float32), (blocks, col_scales))
    proto_grads = proto_parts.reshape(PROTOS, D)
    grad_embeddings = clip_inverse * (clip_grads - normalized_clips * lax.optimization_barrier(jnp.sum(normalized_clips * clip_grads, axis=1, keepdims=True)))
    grad_prototypes = proto_inverse * (proto_grads - unit_protos * lax.optimization_barrier(jnp.sum(unit_protos * proto_grads, axis=1, keepdims=True)))
    return (grad_embeddings, grad_prototypes)
```

```python
import functools

import jax
import jax.numpy as jnp
from jax import lax
from jax.experimental import pallas as pl
from jax.experimental.pallas import tpu as pltpu
from jax.sharding import PartitionSpec as P

LANES = 128
PAIR = 2 * LANES
CHUNK = 64
VMEM_BYTES = 24 * 1024 * 1024


def unit_rows(values):
    inverse = 1.0 / jnp.sqrt(jnp.sum(values * values, axis=1, keepdims=True) + 1e-06)
    return (values * inverse, inverse)


def split(values):
    high = values.astype(jnp.bfloat16)
    low = (values - high.astype(jnp.float32)).astype(jnp.bfloat16)
    return high, low


def dot(left, right):
    return jnp.dot(left, right, preferred_element_type=jnp.float32)


def dot_rows(left, right):
    return lax.dot_general(left, right, (((1,), (1,)), ((), ())), preferred_element_type=jnp.float32)


def call(body, out_shape, **kwargs):
    return pl.pallas_call(
        body, out_shape=out_shape, compiler_params=pltpu.CompilerParams(vmem_limit_bytes=VMEM_BYTES), **kwargs
    )


def f32(*shape):
    return jax.ShapeDtypeStruct(shape, jnp.float32)


def exponents(proto_pair, clips):
    high, low = split(clips)
    scores = dot_rows(proto_pair, jnp.concatenate([high, high], axis=1))
    scores = scores + dot_rows(proto_pair, jnp.concatenate([low, low], axis=1))
    return jnp.exp(scores * 10.0)


def scores_body(protos_ref, clips_ref, e_ref, part_ref, total_ref, x_ref):
    protos = protos_ref[...]
    pair = jnp.concatenate(split(protos), axis=1)
    turned_high, turned_low = split(protos.T)
    turned = jnp.concatenate([turned_high, turned_low], axis=0)
    for block in range(clips_ref.shape[0] // PAIR):
        cols = slice(block * PAIR, (block + 1) * PAIR)
        e = exponents(pair, clips_ref[cols, :])
        e_ref[:, cols] = e
        kernel = e * e
        both = kernel[:, :LANES] + kernel[:, LANES:]
        part_ref[...] = both if block == 0 else part_ref[...] + both
        totals = jnp.sum(e, axis=0, keepdims=True)
        high, low = split(e)
        x = dot(turned, high)
        x = x[:LANES] + x[LANES:] + dot(turned_high, low)
        for half in range(2):
            total_ref[2 * block + half : 2 * block + half + 1, :] = totals[:, half * LANES : (half + 1) * LANES]
            x_ref[2 * block + half] = x[:, half * LANES : (half + 1) * LANES]


def mates_body(index_ref, core_ref, protos_ref, own_ref, other_ref, e_ref, table_ref, mate_ref):
    rows = own_ref.shape[0]
    table_ref[:rows] = own_ref[...]
    table_ref[rows:] = other_ref[...]
    pair = jnp.concatenate(split(protos_ref[...]), axis=1)
    tiles = rows // LANES
    core = core_ref[0]
    for block in range(rows // PAIR):
        for half in range(2):
            tile = 2 * block + half

            def fetch(z, carry, tile=tile, half=half):
                start = (z * tiles + tile) * 16 + core * 8
                base = pl.multiple_of(half * LANES + z * 8, 8)
                picked = [table_ref[pl.ds(index_ref[start + r], 1), :] for r in range(8)]
                mate_ref[pl.ds(base, 8), :] = jnp.concatenate(picked, axis=0)
                return carry

            lax.fori_loop(0, LANES // 8, fetch, 0)
        e_ref[:, block * PAIR : (block + 1) * PAIR] = exponents(pair, mate_ref[...])


def column_scale(own_ref, other_ref, protos):
    half = own_ref.shape[0] // 2
    part = jnp.concatenate([own_ref[:half] + other_ref[half:], own_ref[half:] + other_ref[:half]], axis=0)
    return 1.0 / (protos * jnp.sum(part, axis=1, keepdims=True))


def row_mass(e_ref, scale, tile):
    e = e_ref[:, tile * LANES : (tile + 1) * LANES]
    return jnp.sum(e * e * scale, axis=0, keepdims=True)


def rows_body(protos, e_ref, own_ref, other_ref, *rest):
    *extra, out_ref = rest
    scale = jnp.broadcast_to(column_scale(own_ref, other_ref, protos), own_ref.shape)
    blocks, _, _ = out_ref.shape
    tiles = e_ref.shape[1] // LANES
    masses = jnp.concatenate([row_mass(e_ref, scale, tile) for tile in range(tiles)], axis=0)
    for block in range(blocks):
        out_ref[block, :tiles] = masses
        for ref in extra:
            out_ref[block, tiles:] = ref[...]


def cols_body(clips, e_ref, mass_ref, part_ref):
    tiles = e_ref.shape[1] // LANES
    scale = 1.0 / (clips * jnp.sum(mass_ref[:, :tiles, :], axis=0))
    for start in range(0, e_ref.shape[0], CHUNK):
        rows = slice(start, start + CHUNK)
        total = None
        for tile in range(tiles):
            e = e_ref[rows, tile * LANES : (tile + 1) * LANES]
            term = e * e * scale[tile : tile + 1, :]
            total = term if total is None else total + term
        part_ref[rows, :] = total


def mates_rows_body(protos, mate_e_ref, own_ref, other_ref, protos_ref, x_ref, totals_ref, out_ref, scale_ref):
    scale = jnp.broadcast_to(column_scale(own_ref, other_ref, protos), own_ref.shape)
    scale_ref[...] = scale
    wide = jnp.concatenate([scale, scale], axis=1)
    turned_high, turned_low = split(protos_ref[...].T)
    turned = jnp.concatenate([turned_high, turned_low], axis=0)
    tiles = mate_e_ref.shape[1] // LANES
    totals = 1.0 / totals_ref[...]
    masses = []
    for block in range(tiles // 2):
        e = mate_e_ref[:, block * PAIR : (block + 1) * PAIR]
        kernel = e * e * wide
        mass = jnp.sum(kernel, axis=0, keepdims=True)
        high, low = split(kernel)
        y = dot(turned, high)
        y = y[:LANES] + y[LANES:] + dot(turned_high, low)
        for half in range(2):
            tile = 2 * block + half
            lanes = slice(half * LANES, (half + 1) * LANES)
            masses.append(mass[:, lanes])
            out_ref[tile, :LANES] = x_ref[tile] * totals[tile : tile + 1, :]
            out_ref[tile, LANES : 2 * LANES] = y[:, lanes]
    masses = jnp.concatenate(masses, axis=0)
    for tile in range(tiles):
        out_ref[tile, 2 * LANES :] = masses


def turn_body(in_ref, out_ref):
    total = jnp.sum(in_ref[...], axis=0)
    x = total[:LANES].T
    y = total[LANES : 2 * LANES].T
    masses = total[2 * LANES :]
    for z in range(out_ref.shape[0]):
        out_ref[z, :8] = x[z * 8 : z * 8 + 8]
        out_ref[z, 8:16] = y[z * 8 : z * 8 + 8]
        out_ref[z, 16:] = masses


def grads_body(place_ref, e_ref, mate_e_ref, scale_ref, totals_ref, parts_ref, clips_ref, units_ref, inverse_ref,
               clip_ref, own_ref, other_ref, mass_ref):
    sums = jnp.sum(parts_ref[...], axis=0)
    mass_ref[...] = 1.0 / sums[16:]
    masses = mass_ref[...]
    totals = 1.0 / totals_ref[...]
    tiles = e_ref.shape[1] // LANES
    scale = scale_ref[...]
    acc = None
    for block in range(tiles // 2):
        pieces = []
        for half in range(2):
            tile = 2 * block + half
            lanes = slice(tile * LANES, (tile + 1) * LANES)
            mate = mate_e_ref[:, lanes]
            pieces.append(e_ref[:, lanes] * totals[tile : tile + 1, :] - mate * mate * scale * masses[tile : tile + 1, :])
        high, low = split(jnp.concatenate(pieces, axis=1))
        clip_high, clip_low = split(clips_ref[block * PAIR : (block + 1) * PAIR, :])
        term = dot(high, jnp.concatenate([clip_high, clip_low], axis=1))
        term = term[:, :LANES] + term[:, LANES:] + dot(low, clip_high)
        acc = term if acc is None else acc + term
    acc = acc * 10.0
    half = own_ref.shape[0]
    own_ref[...] = acc[:half]
    other_ref[...] = acc[half:]
    row = jnp.broadcast_to(mass_ref[pl.ds(place_ref[0], 1), :], (8, LANES))
    lane = lax.broadcasted_iota(jnp.int32, (8, LANES), 1)
    line = lax.broadcasted_iota(jnp.int32, (8, LANES), 0)
    own_mass = jnp.sum(jnp.where(lane == place_ref[1] * 8 + line, row, 0.0), axis=1, keepdims=True)
    grads = 10.0 * (sums[:8] - sums[8:16] * own_mass)
    units = units_ref[...]
    clip_ref[...] = inverse_ref[...] * (grads - units * jnp.sum(units * grads, axis=1, keepdims=True))


def local(embeddings, prototypes, partner):
    n_batch, n_proto = lax.axis_size("batch"), lax.axis_size("proto")
    n_chip = n_proto // 2
    rows, features = embeddings.shape
    own_protos = prototypes.shape[0]
    clips, protos = rows * n_batch * n_proto, own_protos * n_batch * n_proto
    here, tiles = n_chip * LANES, n_chip
    core = lax.axis_index("proto") % 2
    chip = lax.axis_index("proto") // 2
    layer = lax.axis_index("batch")
    same_core = [[2 * i + c for i in range(n_chip)] for c in range(2)]
    cores = [(i, i ^ 1) for i in range(n_proto)]
    smem = pl.BlockSpec(memory_space=pltpu.SMEM)
    vmem = pl.BlockSpec(memory_space=pltpu.VMEM)

    def swap(values):
        return lax.ppermute(values, "proto", cores)

    def over_chips(blocks):
        return lax.all_to_all(blocks, "proto", 0, 0, tiled=True, axis_index_groups=same_core)

    def over_layers(blocks):
        return lax.all_to_all(blocks, "batch", 0, 0, tiled=True)

    def summed(blocks):
        part = jnp.sum(over_chips(blocks), axis=0)
        return over_layers(jnp.broadcast_to(part[None], (n_batch,) + part.shape))

    units, inverse = unit_rows(embeddings)
    own_units, proto_inverse = unit_rows(prototypes)
    unit_protos = jnp.concatenate([own_units, swap(own_units)], axis=0)

    line, slot, z = partner % rows, (partner // rows) % n_proto, partner // (rows * n_proto)
    place = (slot % 2) * here + (slot // 2) * LANES + z * rows + line
    place = place.astype(jnp.float32).reshape(n_proto * rows // LANES, LANES)
    block = jnp.concatenate([units, jnp.pad(place, ((0, 8 - place.shape[0]), (0, 0)))], axis=0)
    column = over_layers(jnp.broadcast_to(block[None], (n_batch,) + block.shape))
    places = column[:, rows : rows + place.shape[0]].reshape(-1).astype(jnp.int32)
    places = jnp.where(places >= here, places - here, places + here) * core + places * (1 - core)
    column = column[:, :rows].reshape(LANES, features)
    own_clips = over_chips(jnp.broadcast_to(column[None], (n_chip, LANES, features))).reshape(here, features)
    other_clips = swap(own_clips)

    n_here = 2 * own_protos
    e, part, totals, x = call(
        scores_body, (f32(n_here, here), f32(n_here, LANES), f32(tiles, LANES), f32(tiles, features, LANES))
    )(unit_protos, own_clips)
    mate_e = call(
        mates_body,
        f32(n_here, here),
        in_specs=[smem, smem, vmem, vmem, vmem],
        scratch_shapes=[pltpu.VMEM((2 * here, features), jnp.float32), pltpu.VMEM((PAIR, features), jnp.float32)],
    )(places, core.reshape(1), unit_protos, own_clips, other_clips)

    cols = call(functools.partial(cols_body, float(clips)), f32(n_here, LANES))
    blocks = call(functools.partial(rows_body, float(protos)), f32(n_chip, 2 * tiles, LANES))(e, part, swap(part), totals)
    masses = summed(blocks)
    totals = jnp.sum(masses[:, tiles:], axis=0)
    part = cols(e, masses)
    blocks = call(functools.partial(rows_body, float(protos)), f32(n_chip, tiles, LANES))(e, part, swap(part))
    part = cols(e, summed(blocks))

    blocks, scale = call(
        functools.partial(mates_rows_body, float(protos)), (f32(n_chip, 2 * features + tiles, LANES), f32(n_here, LANES))
    )(mate_e, part, swap(part), unit_protos, x, totals)
    blocks = call(turn_body, f32(n_batch, 2 * rows + tiles, LANES))(over_chips(blocks))
    grad_embeddings, own_grads, other_grads = call(
        grads_body,
        (f32(rows, features), f32(own_protos, features), f32(own_protos, features)),
        in_specs=[smem] + [vmem] * 8,
        scratch_shapes=[pltpu.VMEM((tiles, LANES), jnp.float32)],
    )(jnp.stack([chip, layer]), e, mate_e, scale, totals, over_layers(blocks), own_clips, units, inverse)
    grads = own_grads + swap(other_grads)
    grad_prototypes = proto_inverse * (grads - own_units * jnp.sum(own_units * grads, axis=1, keepdims=True))
    return (grad_embeddings, grad_prototypes)


def solution(mesh):
    in_specs = (P(("batch", "proto"), None), P(("batch", "proto"), None), P("batch"))
    out_specs = (P(("batch", "proto"), None), P(("batch", "proto"), None))
    return jax.shard_map(local, mesh=mesh, in_specs=in_specs, out_specs=out_specs, check_vma=False)
```

```python
import functools

import jax
import jax.numpy as jnp
from jax import lax
from jax.experimental import pallas as pl
from jax.experimental.pallas import tpu as pltpu
from jax.sharding import PartitionSpec as P

LANES = 128
PAIR = 2 * LANES
CHUNK = 64
VMEM_BYTES = 24 * 1024 * 1024


def inverse_norms(values):
    return 1.0 / jnp.sqrt(jnp.sum(values * values, axis=1, keepdims=True) + 1e-06)


def finish_rows(values, grads):
    inverse = inverse_norms(values)
    units = values * inverse
    return inverse * (grads - units * jnp.sum(units * grads, axis=1, keepdims=True))


def split(values):
    high = values.astype(jnp.bfloat16)
    low = (values - high.astype(jnp.float32)).astype(jnp.bfloat16)
    return high, low


def dot(left, right):
    return jnp.dot(left, right, preferred_element_type=jnp.float32)


def dot_rows(left, right):
    return lax.dot_general(left, right, (((1,), (1,)), ((), ())), preferred_element_type=jnp.float32)


def call(body, out_shape, **kwargs):
    return pl.pallas_call(
        body, out_shape=out_shape, compiler_params=pltpu.CompilerParams(vmem_limit_bytes=VMEM_BYTES), **kwargs
    )


def f32(*shape):
    return jax.ShapeDtypeStruct(shape, jnp.float32)


def exponents(proto_pair, clips):
    high, low = split(clips)
    scores = dot_rows(proto_pair, jnp.concatenate([high, high], axis=1))
    scores = scores + dot_rows(proto_pair, jnp.concatenate([low, low], axis=1))
    return jnp.exp(scores * 10.0)


def scores_body(protos_ref, clips_ref, e_ref, part_ref, total_ref, x_ref):
    protos = protos_ref[...]
    pair = jnp.concatenate(split(protos), axis=1)
    turned_high, turned_low = split(protos.T)
    turned = jnp.concatenate([turned_high, turned_low], axis=0)
    for block in range(clips_ref.shape[0] // PAIR):
        cols = slice(block * PAIR, (block + 1) * PAIR)
        e = exponents(pair, clips_ref[cols, :])
        e_ref[:, cols] = e
        kernel = e * e
        both = kernel[:, :LANES] + kernel[:, LANES:]
        part_ref[...] = both if block == 0 else part_ref[...] + both
        totals = jnp.sum(e, axis=0, keepdims=True)
        high, low = split(e)
        x = dot(turned, high)
        x = x[:LANES] + x[LANES:] + dot(turned_high, low)
        for half in range(2):
            total_ref[2 * block + half : 2 * block + half + 1, :] = totals[:, half * LANES : (half + 1) * LANES]
            x_ref[2 * block + half] = x[:, half * LANES : (half + 1) * LANES]


def mates_body(index_ref, spot_ref, protos_ref, own_ref, other_ref, e_ref, table_ref, mate_ref):
    rows = own_ref.shape[0]
    table_ref[:rows] = own_ref[...]
    table_ref[rows:] = other_ref[...]
    pair = jnp.concatenate(split(protos_ref[...]), axis=1)
    tiles = rows // LANES
    first = spot_ref[2] * 8
    for block in range(rows // PAIR):
        slot = block % 2
        for half in range(2):
            for z in range(LANES // 8):
                start = first + (z * tiles + 2 * block + half) * 16
                for r in range(8):
                    mate_ref[slot, half * LANES + z * 8 + r : half * LANES + z * 8 + r + 1, :] = table_ref[
                        pl.ds(index_ref[start + r], 1), :
                    ]
        e_ref[:, block * PAIR : (block + 1) * PAIR] = exponents(pair, mate_ref[slot])


def column_scale(own_ref, other_ref, protos):
    half = own_ref.shape[0] // 2
    part = jnp.concatenate([own_ref[:half] + other_ref[half:], own_ref[half:] + other_ref[:half]], axis=0)
    return 1.0 / (protos * jnp.sum(part, axis=1, keepdims=True))


def row_mass(e_ref, scale, tile):
    e = e_ref[:, tile * LANES : (tile + 1) * LANES]
    return jnp.sum(e * e * scale, axis=0, keepdims=True)


def units_body(in_ref, out_ref):
    values = in_ref[...]
    out_ref[...] = values * inverse_norms(values)


def send_body(n_proto, embeddings_ref, partner_ref, out_ref):
    values = embeddings_ref[...]
    partner = partner_ref[...]
    rows = values.shape[0]
    line = partner & (rows - 1)
    slot = (partner // rows) & (n_proto - 1)
    place = (slot & 1) * (n_proto // 2) + (slot >> 1)
    place = place * LANES + partner // (rows * n_proto) * rows + line
    units = values * inverse_norms(values)
    for layer in range(out_ref.shape[0]):
        out_ref[layer, :rows] = units
        out_ref[layer, rows : rows + place.shape[0]] = place.astype(jnp.float32)
        out_ref[layer, rows + place.shape[0] :] = jnp.zeros((8 - place.shape[0], LANES), jnp.float32)


def column_body(spot_ref, in_ref, out_ref, places_ref):
    n_layers, _, _ = in_ref.shape
    per_layer = places_ref.shape[1]
    for layer in range(n_layers):
        units = in_ref[layer, :8]
        for block in range(out_ref.shape[0]):
            out_ref[block, layer * 8 : layer * 8 + 8] = units
    here = out_ref.shape[0] * LANES
    places = in_ref[:, 8 : 8 + per_layer, :].astype(jnp.int32)
    moved = jnp.where(places >= here, places - here, places + here)
    places_ref[...] = jnp.where(spot_ref[2] > 0, moved, places)


def masses_of(e_ref, scale):
    tiles = e_ref.shape[1] // LANES
    return jnp.concatenate([row_mass(e_ref, scale, tile) for tile in range(tiles)], axis=0)


def rows_first_body(protos, e_ref, own_ref, other_ref, totals_ref, out_ref):
    tiles = e_ref.shape[1] // LANES
    scale = jnp.broadcast_to(column_scale(own_ref, other_ref, protos), own_ref.shape)
    masses = masses_of(e_ref, scale)
    for block in range(tiles):
        out_ref[block, :tiles] = masses
        out_ref[block, tiles:] = jnp.broadcast_to(totals_ref[block : block + 1, :], (8, LANES))


def spread_first_body(in_ref, out_ref):
    tiles = in_ref.shape[0]
    total = jnp.sum(in_ref[...], axis=0)
    size = tiles + 1
    for layer in range(out_ref.shape[0] // size):
        out_ref[layer * size : (layer + 1) * size] = total[:size]


def weigh_columns(e_ref, scale, part_ref):
    tiles = e_ref.shape[1] // LANES
    for start in range(0, e_ref.shape[0], CHUNK):
        rows = slice(start, start + CHUNK)
        total = None
        for tile in range(tiles):
            e = e_ref[rows, tile * LANES : (tile + 1) * LANES]
            term = e * e * scale[tile : tile + 1, :]
            total = term if total is None else total + term
        part_ref[rows, :] = total


def cols_first_body(clips, e_ref, in_ref, part_ref, own_total_ref):
    tiles = e_ref.shape[1] // LANES
    size = tiles + 1
    total = in_ref[:size]
    for layer in range(1, in_ref.shape[0] // size):
        total = total + in_ref[layer * size : (layer + 1) * size]
    own_total_ref[...] = jnp.broadcast_to(total[tiles:], (8, LANES))
    weigh_columns(e_ref, 1.0 / (clips * total[:tiles]), part_ref)


def rows_second_body(protos, e_ref, own_ref, other_ref, x_ref, own_total_ref, out_ref):
    tiles = e_ref.shape[1] // LANES
    scale = jnp.broadcast_to(column_scale(own_ref, other_ref, protos), own_ref.shape)
    masses = masses_of(e_ref, scale)
    for block in range(tiles):
        out_ref[block, :tiles] = masses
        out_ref[block, tiles : tiles + LANES] = x_ref[block]
        out_ref[block, tiles + LANES :] = own_total_ref[...]


def spread_second_body(in_ref, out_ref, x_ref, totals_ref):
    tiles = in_ref.shape[0]
    masses = jnp.sum(in_ref[:, :tiles, :], axis=0)
    for layer in range(out_ref.shape[0] // tiles):
        out_ref[layer * tiles : (layer + 1) * tiles] = masses
    x_ref[...] = jnp.sum(in_ref[:, tiles : tiles + LANES, :], axis=0)
    for block in range(tiles):
        totals_ref[block : block + 1, :] = in_ref[block, tiles + LANES : tiles + LANES + 1, :]


def cols_second_body(clips, e_ref, in_ref, part_ref):
    tiles = e_ref.shape[1] // LANES
    total = in_ref[:tiles]
    for layer in range(1, in_ref.shape[0] // tiles):
        total = total + in_ref[layer * tiles : (layer + 1) * tiles]
    weigh_columns(e_ref, 1.0 / (clips * total), part_ref)


def mates_rows_body(protos, mate_e_ref, own_ref, other_ref, protos_ref, out_ref, scale_ref):
    scale = jnp.broadcast_to(column_scale(own_ref, other_ref, protos), own_ref.shape)
    scale_ref[...] = scale
    wide = jnp.concatenate([scale, scale], axis=1)
    turned_high, turned_low = split(protos_ref[...].T)
    turned = jnp.concatenate([turned_high, turned_low], axis=0)
    tiles = mate_e_ref.shape[1] // LANES
    masses = []
    for block in range(tiles // 2):
        e = mate_e_ref[:, block * PAIR : (block + 1) * PAIR]
        kernel = e * e * wide
        mass = jnp.sum(kernel, axis=0, keepdims=True)
        high, low = split(kernel)
        y = dot(turned, high)
        y = y[:LANES] + y[LANES:] + dot(turned_high, low)
        for half in range(2):
            lanes = slice(half * LANES, (half + 1) * LANES)
            masses.append(mass[:, lanes])
            out_ref[2 * block + half, :LANES] = y[:, lanes]
    masses = jnp.concatenate(masses, axis=0)
    for tile in range(tiles):
        out_ref[tile, LANES:] = masses


def turn_body(in_ref, x_ref, own_total_ref, out_ref):
    tiles = in_ref.shape[0]
    size = 16 + tiles
    total = jnp.sum(in_ref[...], axis=0)
    x = (x_ref[...] / own_total_ref[0:1, :]).T
    y = total[:LANES].T
    masses = total[LANES:]
    for layer in range(out_ref.shape[0] // size):
        base = layer * size
        out_ref[base : base + 8] = x[layer * 8 : layer * 8 + 8]
        out_ref[base + 8 : base + 16] = y[layer * 8 : layer * 8 + 8]
        out_ref[base + 16 : base + size] = masses


def grads_body(spot_ref, e_ref, mate_e_ref, scale_ref, totals_ref, in_ref, clips_ref, embeddings_ref,
               clip_ref, own_ref, other_ref, mass_ref):
    tiles = e_ref.shape[1] // LANES
    size = 16 + tiles
    sums = in_ref[:size]
    for layer in range(1, in_ref.shape[0] // size):
        sums = sums + in_ref[layer * size : (layer + 1) * size]
    mass_ref[...] = 1.0 / sums[16:]
    masses = mass_ref[...]
    totals = 1.0 / totals_ref[...]
    scale = scale_ref[...]
    acc = None
    for block in range(tiles // 2):
        pieces = []
        for half in range(2):
            tile = 2 * block + half
            lanes = slice(tile * LANES, (tile + 1) * LANES)
            mate = mate_e_ref[:, lanes]
            pieces.append(e_ref[:, lanes] * totals[tile : tile + 1, :] - mate * mate * scale * masses[tile : tile + 1, :])
        high, low = split(jnp.concatenate(pieces, axis=1))
        clip_high, clip_low = split(clips_ref[block * PAIR : (block + 1) * PAIR, :])
        term = dot(high, jnp.concatenate([clip_high, clip_low], axis=1))
        term = term[:, :LANES] + term[:, LANES:] + dot(low, clip_high)
        acc = term if acc is None else acc + term
    acc = acc * 10.0
    half = own_ref.shape[0]
    own_ref[...] = acc[:half]
    other_ref[...] = acc[half:]
    row = jnp.broadcast_to(mass_ref[pl.ds(spot_ref[0], 1), :], (8, LANES))
    lane = lax.broadcasted_iota(jnp.int32, (8, LANES), 1)
    line = lax.broadcasted_iota(jnp.int32, (8, LANES), 0)
    own_mass = jnp.sum(jnp.where(lane == spot_ref[1] * 8 + line, row, 0.0), axis=1, keepdims=True)
    clip_ref[...] = finish_rows(embeddings_ref[...], 10.0 * (sums[:8] - sums[8:16] * own_mass))


def finish_body(protos_ref, own_ref, other_ref, out_ref):
    out_ref[...] = finish_rows(protos_ref[...], own_ref[...] + other_ref[...])


def local(embeddings, prototypes, partner):
    n_batch, n_proto = lax.axis_size("batch"), lax.axis_size("proto")
    tiles = n_proto // 2
    rows, features = embeddings.shape
    own_protos = prototypes.shape[0]
    clips, protos = float(rows * n_batch * n_proto), float(own_protos * n_batch * n_proto)
    here, n_here = tiles * LANES, 2 * own_protos
    where = lax.axis_index("proto")
    same_core = [[2 * i + c for i in range(tiles)] for c in range(2)]
    cores = [(i, i ^ 1) for i in range(n_proto)]
    smem = pl.BlockSpec(memory_space=pltpu.SMEM)
    vmem = pl.BlockSpec(memory_space=pltpu.VMEM)

    def swap(values):
        return lax.ppermute(values, "proto", cores)

    def over_chips(blocks):
        return lax.all_to_all(blocks, "proto", 0, 0, tiled=True, axis_index_groups=same_core)

    def over_layers(lines):
        blocks = lax.all_to_all(lines.reshape(n_batch, 1, -1), "batch", 0, 0, tiled=True)
        return blocks.reshape(lines.shape)

    spot = jnp.stack([where >> 1, lax.axis_index("batch"), where & 1])
    partner = partner.reshape(-1, LANES)
    sent = call(functools.partial(send_body, n_proto), f32(n_batch, rows + 8, LANES))(embeddings, partner)
    sent, held, spot = lax.optimization_barrier((sent, prototypes, spot))
    column = lax.all_to_all(sent, "batch", 0, 0, tiled=True)
    own_units = call(units_body, f32(own_protos, features))(held)
    unit_protos = jnp.concatenate([own_units, swap(own_units)], axis=0)
    column, unit_protos = lax.optimization_barrier((column, unit_protos))
    blocks, places = call(
        column_body,
        (f32(tiles, LANES, features), jax.ShapeDtypeStruct((n_batch, partner.shape[0], LANES), jnp.int32)),
        in_specs=[smem, vmem],
    )(spot, column)
    own_clips = over_chips(blocks).reshape(here, features)
    other_clips = swap(own_clips)

    e, part, totals, x = call(
        scores_body, (f32(n_here, here), f32(n_here, LANES), f32(tiles, LANES), f32(tiles, features, LANES))
    )(unit_protos, own_clips)
    part, other_clips = lax.optimization_barrier((part, other_clips))
    mate_e = call(
        mates_body,
        f32(n_here, here),
        in_specs=[smem, smem, vmem, vmem, vmem],
        scratch_shapes=[pltpu.VMEM((2 * here, features), jnp.float32), pltpu.VMEM((2, PAIR, features), jnp.float32)],
    )(places.reshape(-1), spot, unit_protos, own_clips, other_clips)

    blocks = call(functools.partial(rows_first_body, protos), f32(tiles, tiles + 8, LANES))(e, part, swap(part), totals)
    lines = call(spread_first_body, f32(n_batch * (tiles + 1), LANES))(over_chips(blocks))
    part, own_total = call(functools.partial(cols_first_body, clips), (f32(n_here, LANES), f32(8, LANES)))(
        e, over_layers(lines)
    )
    blocks = call(functools.partial(rows_second_body, protos), f32(tiles, tiles + LANES + 8, LANES))(
        e, part, swap(part), x, own_total
    )
    lines, x, totals = call(
        spread_second_body, (f32(n_batch * tiles, LANES), f32(features, LANES), f32(tiles, LANES))
    )(over_chips(blocks))
    part = call(functools.partial(cols_second_body, clips), f32(n_here, LANES))(e, over_layers(lines))
    blocks, scale = call(
        functools.partial(mates_rows_body, protos), (f32(tiles, features + tiles, LANES), f32(n_here, LANES))
    )(mate_e, part, swap(part), unit_protos)
    lines = call(turn_body, f32(n_batch * (16 + tiles), LANES))(over_chips(blocks), x, own_total)
    grad_embeddings, own_grads, other_grads = call(
        grads_body,
        (f32(rows, features), f32(own_protos, features), f32(own_protos, features)),
        in_specs=[smem] + [vmem] * 7,
        scratch_shapes=[pltpu.VMEM((tiles, LANES), jnp.float32)],
    )(spot, e, mate_e, scale, totals, over_layers(lines), own_clips, embeddings)
    grad_prototypes = call(finish_body, f32(own_protos, features))(prototypes, own_grads, swap(other_grads))
    return (grad_embeddings, grad_prototypes)


def solution(mesh):
    in_specs = (P(("batch", "proto"), None), P(("batch", "proto"), None), P("batch"))
    out_specs = (P(("batch", "proto"), None), P(("batch", "proto"), None))
    return jax.shard_map(local, mesh=mesh, in_specs=in_specs, out_specs=out_specs, check_vma=False)
```

```python
import functools

import jax
import jax.numpy as jnp
from jax import lax
from jax.experimental import pallas as pl
from jax.experimental.pallas import tpu as pltpu
from jax.sharding import PartitionSpec as P

LANES = 128
PAIR = 2 * LANES
CHUNK = 64
VMEM_BYTES = 24 * 1024 * 1024


def inverse_norms(values):
    return 1.0 / jnp.sqrt(jnp.sum(values * values, axis=1, keepdims=True) + 1e-06)


def finish_rows(values, grads):
    inverse = inverse_norms(values)
    units = values * inverse
    return inverse * (grads - units * jnp.sum(units * grads, axis=1, keepdims=True))


def split(values):
    high = values.astype(jnp.bfloat16)
    low = (values - high.astype(jnp.float32)).astype(jnp.bfloat16)
    return high, low


def dot(left, right):
    return jnp.dot(left, right, preferred_element_type=jnp.float32)


def dot_rows(left, right):
    return lax.dot_general(left, right, (((1,), (1,)), ((), ())), preferred_element_type=jnp.float32)


def call(body, out_shape, **kwargs):
    return pl.pallas_call(
        body, out_shape=out_shape, compiler_params=pltpu.CompilerParams(vmem_limit_bytes=VMEM_BYTES), **kwargs
    )


def f32(*shape):
    return jax.ShapeDtypeStruct(shape, jnp.float32)


def exponents(proto_pair, clips):
    high, low = split(clips)
    scores = dot_rows(proto_pair, jnp.concatenate([high, high], axis=1))
    scores = scores + dot_rows(proto_pair, jnp.concatenate([low, low], axis=1))
    return jnp.exp(scores * 10.0)


def scores_body(protos_ref, clips_ref, e_ref, total_ref, bundle_ref):
    n_here = protos_ref.shape[0]
    pair = jnp.concatenate(split(protos_ref[...]), axis=1)
    for block in range(clips_ref.shape[0] // PAIR):
        cols = slice(block * PAIR, (block + 1) * PAIR)
        clips = clips_ref[cols, :]
        bundle_ref[n_here + block * PAIR : n_here + (block + 1) * PAIR] = clips
        e = exponents(pair, clips)
        e_ref[:, cols] = e
        kernel = e * e
        both = kernel[:, :LANES] + kernel[:, LANES:]
        bundle_ref[:n_here] = both if block == 0 else bundle_ref[:n_here] + both
        totals = jnp.sum(e, axis=0, keepdims=True)
        for half in range(2):
            total_ref[2 * block + half : 2 * block + half + 1, :] = totals[:, half * LANES : (half + 1) * LANES]


def turned_protos(protos_ref):
    high, low = split(protos_ref[...].T)
    return jnp.concatenate([high, low], axis=0)


def times_protos(turned, weights):
    high, low = split(weights)
    both = dot(turned, high)
    return both[:LANES] + both[LANES:] + dot(turned[:LANES], low)


def pulls_body(protos_ref, e_ref, x_ref):
    turned = turned_protos(protos_ref)
    for block in range(e_ref.shape[1] // PAIR):
        x = times_protos(turned, e_ref[:, block * PAIR : (block + 1) * PAIR])
        for half in range(2):
            x_ref[2 * block + half] = x[:, half * LANES : (half + 1) * LANES]


def mates_of(part, index_ref, spot_ref, protos_ref, table_ref, e_ref, mate_ref):
    pair = jnp.concatenate(split(protos_ref[...]), axis=1)
    blocks = e_ref.shape[1] // PAIR
    tiles = 4 * blocks
    first = spot_ref[2] * 8
    for block in range(blocks):
        slot = block % 2
        for half in range(2):
            for z in range(LANES // 8):
                start = first + (z * tiles + 2 * (part * blocks + block) + half) * 16
                for r in range(8):
                    row = half * LANES + z * 8 + r
                    mate_ref[slot, row : row + 1, :] = table_ref[pl.ds(index_ref[start + r], 1), :]
        e_ref[:, block * PAIR : (block + 1) * PAIR] = exponents(pair, mate_ref[slot])


def mates_first_body(index_ref, spot_ref, protos_ref, own_ref, other_ref, e_ref, table_ref, mate_ref):
    rows = own_ref.shape[0]
    table_ref[:rows] = own_ref[...]
    table_ref[rows:] = other_ref[protos_ref.shape[0] :]
    mates_of(0, index_ref, spot_ref, protos_ref, table_ref, e_ref, mate_ref)


def mates_second_body(index_ref, spot_ref, protos_ref, table_ref, e_ref, mate_ref):
    mates_of(1, index_ref, spot_ref, protos_ref, table_ref, e_ref, mate_ref)


def column_scale(own_ref, other_ref, rows, protos):
    half = rows // 2
    part = jnp.concatenate([own_ref[:half] + other_ref[half:rows], own_ref[half:rows] + other_ref[:half]], axis=0)
    scale = 1.0 / (protos * jnp.sum(part, axis=1, keepdims=True))
    return jnp.broadcast_to(scale, (rows, LANES))


def row_mass(e_ref, scale, tile):
    e = e_ref[:, tile * LANES : (tile + 1) * LANES]
    return jnp.sum(e * e * scale, axis=0, keepdims=True)


def units_body(in_ref, out_ref):
    values = in_ref[...]
    out_ref[...] = values * inverse_norms(values)


def send_body(n_proto, embeddings_ref, partner_ref, out_ref, values_ref, mates_ref, sems):
    copies = [
        pltpu.make_async_copy(embeddings_ref, values_ref, sems.at[0]),
        pltpu.make_async_copy(partner_ref, mates_ref, sems.at[1]),
    ]
    for copy in copies:
        copy.start()
    for copy in copies:
        copy.wait()
    values = values_ref[...]
    partner = mates_ref[...]
    rows = values.shape[0]
    line = partner & (rows - 1)
    slot = (partner // rows) & (n_proto - 1)
    place = (slot & 1) * (n_proto // 2) + (slot >> 1)
    place = place * LANES + partner // (rows * n_proto) * rows + line
    block = jnp.concatenate([values * inverse_norms(values), place.astype(jnp.float32)], axis=0)
    for layer in range(out_ref.shape[0] // block.shape[0]):
        out_ref[layer * block.shape[0] : (layer + 1) * block.shape[0]] = block


def column_body(spot_ref, in_ref, out_ref, places_ref):
    per_layer = places_ref.shape[1]
    size = 8 + per_layer
    places = []
    for layer in range(places_ref.shape[0]):
        units = in_ref[layer * size : layer * size + 8]
        places.append(in_ref[layer * size + 8 : (layer + 1) * size][None])
        for block in range(out_ref.shape[0]):
            out_ref[block, layer * 8 : layer * 8 + 8] = units
    here = out_ref.shape[0] * LANES
    places = jnp.concatenate(places, axis=0).astype(jnp.int32)
    moved = jnp.where(places >= here, places - here, places + here)
    places_ref[...] = jnp.where(spot_ref[2] > 0, moved, places)


def masses_of(e_ref, scale):
    tiles = e_ref.shape[1] // LANES
    return jnp.concatenate([row_mass(e_ref, scale, tile) for tile in range(tiles)], axis=0)


def rows_first_body(protos, e_ref, own_ref, other_ref, totals_ref, out_ref):
    tiles = e_ref.shape[1] // LANES
    scale = column_scale(own_ref, other_ref, e_ref.shape[0], protos)
    masses = masses_of(e_ref, scale)
    for block in range(tiles):
        out_ref[block, :tiles] = masses
        out_ref[block, tiles:] = jnp.broadcast_to(totals_ref[block : block + 1, :], (8, LANES))


def spread_first_body(in_ref, out_ref):
    tiles = in_ref.shape[0]
    total = jnp.sum(in_ref[...], axis=0)
    size = tiles + 1
    for layer in range(out_ref.shape[0] // size):
        out_ref[layer * size : (layer + 1) * size] = total[:size]


def weigh_columns(e_ref, scale, part_ref):
    tiles = e_ref.shape[1] // LANES
    for start in range(0, e_ref.shape[0], CHUNK):
        rows = slice(start, start + CHUNK)
        total = None
        for tile in range(tiles):
            e = e_ref[rows, tile * LANES : (tile + 1) * LANES]
            term = e * e * scale[tile : tile + 1, :]
            total = term if total is None else total + term
        part_ref[rows, :] = total


def cols_first_body(clips, e_ref, in_ref, part_ref, own_total_ref):
    tiles = e_ref.shape[1] // LANES
    size = tiles + 1
    total = in_ref[:size]
    for layer in range(1, in_ref.shape[0] // size):
        total = total + in_ref[layer * size : (layer + 1) * size]
    own_total_ref[...] = jnp.broadcast_to(total[tiles:], (8, LANES))
    weigh_columns(e_ref, 1.0 / (clips * total[:tiles]), part_ref)


def rows_second_body(protos, e_ref, own_ref, other_ref, x_ref, own_total_ref, out_ref):
    tiles = e_ref.shape[1] // LANES
    scale = column_scale(own_ref, other_ref, e_ref.shape[0], protos)
    masses = masses_of(e_ref, scale)
    for block in range(tiles):
        out_ref[block, :tiles] = masses
        out_ref[block, tiles : tiles + LANES] = x_ref[block]
        out_ref[block, tiles + LANES :] = own_total_ref[...]


def spread_second_body(in_ref, out_ref, totals_ref):
    tiles = in_ref.shape[0]
    size = tiles + 8
    total = jnp.sum(in_ref[:, : tiles + LANES, :], axis=0)
    x = total[tiles:].T
    for layer in range(out_ref.shape[0] // size):
        base = layer * size
        out_ref[base : base + tiles] = total[:tiles]
        out_ref[base + tiles : base + size] = x[layer * 8 : layer * 8 + 8]
    for block in range(tiles):
        totals_ref[block : block + 1, :] = in_ref[block, tiles + LANES : tiles + LANES + 1, :]


def summed_lines(in_ref, size):
    total = in_ref[:size]
    for layer in range(1, in_ref.shape[0] // size):
        total = total + in_ref[layer * size : (layer + 1) * size]
    return total


def cols_second_body(clips, e_ref, in_ref, part_ref, x_ref):
    tiles = e_ref.shape[1] // LANES
    total = summed_lines(in_ref, tiles + 8)
    x_ref[...] = total[tiles:]
    weigh_columns(e_ref, 1.0 / (clips * total[:tiles]), part_ref)


def mates_rows_body(protos, first_ref, second_ref, own_ref, other_ref, protos_ref, out_ref, scale_ref):
    scale = column_scale(own_ref, other_ref, protos_ref.shape[0], protos)
    scale_ref[...] = scale
    wide = jnp.concatenate([scale, scale], axis=1)
    turned = turned_protos(protos_ref)
    masses = []
    blocks = first_ref.shape[1] // PAIR
    for block in range(2 * blocks):
        mate_e_ref = first_ref if block < blocks else second_ref
        start = block % blocks * PAIR
        e = mate_e_ref[:, start : start + PAIR]
        kernel = e * e * wide
        mass = jnp.sum(kernel, axis=0, keepdims=True)
        y = times_protos(turned, kernel)
        for half in range(2):
            lanes = slice(half * LANES, (half + 1) * LANES)
            masses.append(mass[:, lanes])
            out_ref[2 * block + half, :LANES] = y[:, lanes]
    masses = jnp.concatenate(masses, axis=0)
    for tile in range(out_ref.shape[0]):
        out_ref[tile, LANES:] = masses


def turn_body(in_ref, out_ref):
    tiles = in_ref.shape[0]
    size = 8 + tiles
    total = jnp.sum(in_ref[...], axis=0)
    y = total[:LANES].T
    for layer in range(out_ref.shape[0] // size):
        base = layer * size
        out_ref[base : base + 8] = y[layer * 8 : layer * 8 + 8]
        out_ref[base + 8 : base + size] = total[LANES:]


def proto_grads(rows, e_ref, first_ref, second_ref, scale_ref, shares, masses, clips_ref):
    scale = scale_ref[rows, :]
    blocks = first_ref.shape[1] // PAIR
    acc = None
    for block in range(2 * blocks):
        mate_e_ref = first_ref if block < blocks else second_ref
        pieces = []
        for half in range(2):
            tile = 2 * block + half
            mate = mate_e_ref[rows, (block % blocks * 2 + half) * LANES : (block % blocks * 2 + half + 1) * LANES]
            e = e_ref[rows, tile * LANES : (tile + 1) * LANES]
            pieces.append(e * shares[tile : tile + 1, :] - mate * mate * scale * masses[tile : tile + 1, :])
        high, low = split(jnp.concatenate(pieces, axis=1))
        clip_high, clip_low = split(clips_ref[block * PAIR : (block + 1) * PAIR, :])
        term = dot(high, jnp.concatenate([clip_high, clip_low], axis=1))
        term = term[:, :LANES] + term[:, LANES:] + dot(low, clip_high)
        acc = term if acc is None else acc + term
    return acc * 10.0


def other_grads_body(e_ref, first_ref, second_ref, scale_ref, totals_ref, in_ref, clips_ref, out_ref, y_ref, inverse_ref):
    n_rows = out_ref.shape[0]
    tiles = totals_ref.shape[0]
    total = summed_lines(in_ref, 8 + tiles)
    y_ref[...] = total[:8]
    masses = 1.0 / total[8:]
    shares = 1.0 / totals_ref[...]
    inverse_ref[:tiles] = masses
    inverse_ref[tiles:] = shares
    rows = slice(n_rows, 2 * n_rows)
    out_ref[...] = proto_grads(rows, e_ref, first_ref, second_ref, scale_ref, shares, masses, clips_ref)


def own_values(ref, row, layer):
    values = jnp.broadcast_to(ref[pl.ds(row, 1), :], (8, LANES))
    lane = lax.broadcasted_iota(jnp.int32, (8, LANES), 1)
    line = lax.broadcasted_iota(jnp.int32, (8, LANES), 0)
    return jnp.sum(jnp.where(lane == layer * 8 + line, values, 0.0), axis=1, keepdims=True)


def own_grads_body(spot_ref, e_ref, first_ref, second_ref, scale_ref, inverse_ref, x_ref, y_ref, clips_ref,
                   embeddings_ref, clip_ref, out_ref):
    tiles = inverse_ref.shape[0] // 2
    rows = slice(0, out_ref.shape[0])
    out_ref[...] = proto_grads(
        rows, e_ref, first_ref, second_ref, scale_ref, inverse_ref[tiles:], inverse_ref[:tiles], clips_ref
    )
    own_mass = own_values(inverse_ref, spot_ref[0], spot_ref[1])
    own_share = own_values(inverse_ref, spot_ref[0] + tiles, spot_ref[1])
    clip_ref[...] = finish_rows(embeddings_ref[...], 10.0 * (x_ref[...] * own_share - y_ref[...] * own_mass))


def finish_body(protos_ref, own_ref, other_ref, out_ref):
    out_ref[...] = finish_rows(protos_ref[...], own_ref[...] + other_ref[...])


def local(embeddings, prototypes, partner):
    n_batch, n_proto = lax.axis_size("batch"), lax.axis_size("proto")
    tiles = n_proto // 2
    rows, features = embeddings.shape
    own_protos = prototypes.shape[0]
    clips, protos = float(rows * n_batch * n_proto), float(own_protos * n_batch * n_proto)
    here, n_here = tiles * LANES, 2 * own_protos
    where = lax.axis_index("proto")
    same_core = [[2 * i + c for i in range(tiles)] for c in range(2)]
    cores = [(i, i ^ 1) for i in range(n_proto)]
    smem = pl.BlockSpec(memory_space=pltpu.SMEM)
    vmem = pl.BlockSpec(memory_space=pltpu.VMEM)

    def swap(values):
        return lax.ppermute(values, "proto", cores)

    def over_chips(blocks):
        return lax.all_to_all(blocks, "proto", 0, 0, tiled=True, axis_index_groups=same_core)

    def over_layers(lines):
        blocks = lax.all_to_all(lines.reshape(n_batch, 1, -1), "batch", 0, 0, tiled=True)
        return blocks.reshape(lines.shape)

    spot = jnp.stack([where >> 1, lax.axis_index("batch"), where & 1])
    partner = partner.reshape(-1, LANES)
    sent = call(
        functools.partial(send_body, n_proto),
        f32(n_batch * (rows + partner.shape[0]), LANES),
        in_specs=[pl.BlockSpec(memory_space=pltpu.HBM)] * 2,
        scratch_shapes=[
            pltpu.VMEM(embeddings.shape, jnp.float32),
            pltpu.VMEM(partner.shape, jnp.int32),
            pltpu.SemaphoreType.DMA((2,)),
        ],
    )(embeddings, partner)
    sent, held, spot = lax.optimization_barrier((sent, prototypes, spot))
    column = over_layers(sent)
    own_units = call(units_body, f32(own_protos, features))(held)
    unit_protos = jnp.concatenate([own_units, swap(own_units)], axis=0)
    column, unit_protos = lax.optimization_barrier((column, unit_protos))
    blocks, places = call(
        column_body,
        (f32(tiles, LANES, features), jax.ShapeDtypeStruct((n_batch, partner.shape[0], LANES), jnp.int32)),
        in_specs=[smem, vmem],
    )(spot, column)
    own_clips = over_chips(blocks).reshape(here, features)

    e, totals, bundle = call(
        scores_body, (f32(n_here, here), f32(tiles, LANES), f32(n_here + here, features))
    )(unit_protos, own_clips)
    x = call(pulls_body, f32(tiles, features, LANES))(unit_protos, e)
    received, x = lax.optimization_barrier((swap(bundle), x))
    blocks = call(functools.partial(rows_first_body, protos), f32(tiles, tiles + 8, LANES))(e, bundle, received, totals)
    lines = call(spread_first_body, f32(n_batch * (tiles + 1), LANES))(over_chips(blocks))
    part, own_total = call(functools.partial(cols_first_body, clips), (f32(n_here, LANES), f32(8, LANES)))(
        e, over_layers(lines)
    )

    mates = pltpu.VMEM((2, PAIR, features), jnp.float32)
    part, late = lax.optimization_barrier((part, places.reshape(-1)))
    first_e, table = call(
        mates_first_body,
        (f32(n_here, here // 2), f32(2 * here, features)),
        in_specs=[smem, smem, vmem, vmem, vmem],
        scratch_shapes=[mates],
    )(late, spot, unit_protos, own_clips, received)
    other, first_e = lax.optimization_barrier((swap(part), first_e))
    blocks = call(functools.partial(rows_second_body, protos), f32(tiles, tiles + LANES + 8, LANES))(
        e, part, other, x, own_total
    )
    lines, totals = call(spread_second_body, (f32(n_batch * (tiles + 8), LANES), f32(tiles, LANES)))(over_chips(blocks))
    part, x = call(functools.partial(cols_second_body, clips), (f32(n_here, LANES), f32(rows, features)))(
        e, over_layers(lines)
    )
    part, late = lax.optimization_barrier((part, late))
    second_e = call(
        mates_second_body, f32(n_here, here // 2), in_specs=[smem, smem, vmem, vmem], scratch_shapes=[mates]
    )(late, spot, unit_protos, table)
    other, second_e = lax.optimization_barrier((swap(part), second_e))
    blocks, scale = call(
        functools.partial(mates_rows_body, protos), (f32(tiles, features + tiles, LANES), f32(n_here, LANES))
    )(first_e, second_e, part, other, unit_protos)
    lines = call(turn_body, f32(n_batch * (8 + tiles), LANES))(over_chips(blocks))
    other_grads, y, inverse = call(
        other_grads_body, (f32(own_protos, features), f32(rows, features), f32(2 * tiles, LANES))
    )(e, first_e, second_e, scale, totals, over_layers(lines), own_clips)
    grad_embeddings, own_grads = call(
        own_grads_body, (f32(rows, features), f32(own_protos, features)), in_specs=[smem] + [vmem] * 9
    )(spot, e, first_e, second_e, scale, inverse, x, y, own_clips, embeddings)
    grad_prototypes = call(finish_body, f32(own_protos, features))(prototypes, own_grads, swap(other_grads))
    return (grad_embeddings, grad_prototypes)


def solution(mesh):
    in_specs = (P(("batch", "proto"), None), P(("batch", "proto"), None), P("batch"))
    out_specs = (P(("batch", "proto"), None), P(("batch", "proto"), None))
    return jax.shard_map(local, mesh=mesh, in_specs=in_specs, out_specs=out_specs, check_vma=False)
```

```python
import functools

import jax
import jax.numpy as jnp
from jax import lax
from jax.experimental import pallas as pl
from jax.experimental.pallas import tpu as pltpu
from jax.sharding import PartitionSpec as P

LANES = 128
PAIR = 2 * LANES
CHUNK = 64
VMEM_BYTES = 24 * 1024 * 1024


def inverse_norms(values):
    return 1.0 / jnp.sqrt(jnp.sum(values * values, axis=1, keepdims=True) + 1e-06)


def finish_rows(values, grads):
    inverse = inverse_norms(values)
    units = values * inverse
    return inverse * (grads - units * jnp.sum(units * grads, axis=1, keepdims=True))


def split(values):
    high = values.astype(jnp.bfloat16)
    low = (values - high.astype(jnp.float32)).astype(jnp.bfloat16)
    return high, low


def dot(left, right):
    return jnp.dot(left, right, preferred_element_type=jnp.float32)


def dot_rows(left, right):
    return lax.dot_general(left, right, (((1,), (1,)), ((), ())), preferred_element_type=jnp.float32)


def call(body, out_shape, **kwargs):
    return pl.pallas_call(
        body, out_shape=out_shape, compiler_params=pltpu.CompilerParams(vmem_limit_bytes=VMEM_BYTES), **kwargs
    )


def f32(*shape):
    return jax.ShapeDtypeStruct(shape, jnp.float32)


def exponents(proto_pair, clips):
    high, low = split(clips)
    scores = dot_rows(proto_pair, jnp.concatenate([high, high], axis=1))
    scores = scores + dot_rows(proto_pair, jnp.concatenate([low, low], axis=1))
    return jnp.exp(scores * 10.0)


def scores_body(protos_ref, clips_ref, e_ref, total_ref, bundle_ref):
    n_here = protos_ref.shape[0]
    pair = jnp.concatenate(split(protos_ref[...]), axis=1)
    for block in range(clips_ref.shape[0] // PAIR):
        cols = slice(block * PAIR, (block + 1) * PAIR)
        clips = clips_ref[cols, :]
        bundle_ref[n_here + block * PAIR : n_here + (block + 1) * PAIR] = clips
        e = exponents(pair, clips)
        e_ref[:, cols] = e
        kernel = e * e
        both = kernel[:, :LANES] + kernel[:, LANES:]
        bundle_ref[:n_here] = both if block == 0 else bundle_ref[:n_here] + both
        totals = jnp.sum(e, axis=0, keepdims=True)
        for half in range(2):
            total_ref[2 * block + half : 2 * block + half + 1, :] = totals[:, half * LANES : (half + 1) * LANES]


def turned_protos(protos_ref):
    high, low = split(protos_ref[...].T)
    return jnp.concatenate([high, low], axis=0)


def times_protos(turned, weights):
    high, low = split(weights)
    both = dot(turned, high)
    return both[:LANES] + both[LANES:] + dot(turned[:LANES], low)


def pulls_body(protos_ref, e_ref, x_ref):
    turned = turned_protos(protos_ref)
    for block in range(e_ref.shape[1] // PAIR):
        x = times_protos(turned, e_ref[:, block * PAIR : (block + 1) * PAIR])
        for half in range(2):
            x_ref[2 * block + half] = x[:, half * LANES : (half + 1) * LANES]


def mates_of(part, index_ref, spot_ref, protos_ref, table_ref, e_ref, mate_ref):
    pair = jnp.concatenate(split(protos_ref[...]), axis=1)
    blocks = e_ref.shape[1] // PAIR
    tiles = 4 * blocks
    first = spot_ref[2] * 8
    for block in range(blocks):
        slot = block % 2
        for half in range(2):
            for z in range(LANES // 8):
                start = first + (z * tiles + 2 * (part * blocks + block) + half) * 16
                for r in range(8):
                    row = half * LANES + z * 8 + r
                    mate_ref[slot, row : row + 1, :] = table_ref[pl.ds(index_ref[start + r], 1), :]
        e_ref[:, block * PAIR : (block + 1) * PAIR] = exponents(pair, mate_ref[slot])


def mates_first_body(index_ref, spot_ref, protos_ref, own_ref, other_ref, e_ref, table_ref, mate_ref):
    rows = own_ref.shape[0]
    table_ref[:rows] = own_ref[...]
    table_ref[rows:] = other_ref[protos_ref.shape[0] :]
    mates_of(0, index_ref, spot_ref, protos_ref, table_ref, e_ref, mate_ref)


def mates_second_body(index_ref, spot_ref, protos_ref, table_ref, e_ref, mate_ref):
    mates_of(1, index_ref, spot_ref, protos_ref, table_ref, e_ref, mate_ref)


def column_scale(own_ref, other_ref, rows, protos):
    half = rows // 2
    part = jnp.concatenate([own_ref[:half] + other_ref[half:rows], own_ref[half:rows] + other_ref[:half]], axis=0)
    scale = 1.0 / (protos * jnp.sum(part, axis=1, keepdims=True))
    return jnp.broadcast_to(scale, (rows, LANES))


def row_mass(e_ref, scale, tile):
    e = e_ref[:, tile * LANES : (tile + 1) * LANES]
    return jnp.sum(e * e * scale, axis=0, keepdims=True)


def units_body(in_ref, out_ref):
    values = in_ref[...]
    out_ref[...] = values * inverse_norms(values)


def send_body(n_proto, rows, in_ref, out_ref):
    values = in_ref[:rows]
    partner = in_ref[rows:].astype(jnp.int32)
    line = partner & (rows - 1)
    slot = (partner // rows) & (n_proto - 1)
    place = (slot & 1) * (n_proto // 2) + (slot >> 1)
    place = place * LANES + partner // (rows * n_proto) * rows + line
    block = jnp.concatenate([values * inverse_norms(values), place.astype(jnp.float32)], axis=0)
    for layer in range(out_ref.shape[0] // block.shape[0]):
        out_ref[layer * block.shape[0] : (layer + 1) * block.shape[0]] = block


def column_body(spot_ref, in_ref, out_ref, places_ref):
    per_layer = places_ref.shape[1]
    size = 8 + per_layer
    places = []
    for layer in range(places_ref.shape[0]):
        units = in_ref[layer * size : layer * size + 8]
        places.append(in_ref[layer * size + 8 : (layer + 1) * size][None])
        for block in range(out_ref.shape[0]):
            out_ref[block, layer * 8 : layer * 8 + 8] = units
    here = out_ref.shape[0] * LANES
    places = jnp.concatenate(places, axis=0).astype(jnp.int32)
    moved = jnp.where(places >= here, places - here, places + here)
    places_ref[...] = jnp.where(spot_ref[2] > 0, moved, places)


def masses_of(e_ref, scale):
    tiles = e_ref.shape[1] // LANES
    return jnp.concatenate([row_mass(e_ref, scale, tile) for tile in range(tiles)], axis=0)


def rows_first_body(protos, e_ref, own_ref, other_ref, totals_ref, out_ref):
    tiles = e_ref.shape[1] // LANES
    scale = column_scale(own_ref, other_ref, e_ref.shape[0], protos)
    masses = masses_of(e_ref, scale)
    for block in range(tiles):
        out_ref[block, :tiles] = masses
        out_ref[block, tiles:] = jnp.broadcast_to(totals_ref[block : block + 1, :], (8, LANES))


def spread_first_body(in_ref, out_ref):
    tiles = in_ref.shape[0]
    total = jnp.sum(in_ref[...], axis=0)
    size = tiles + 1
    for layer in range(out_ref.shape[0] // size):
        out_ref[layer * size : (layer + 1) * size] = total[:size]


def weigh_columns(e_ref, scale, part_ref):
    tiles = e_ref.shape[1] // LANES
    for start in range(0, e_ref.shape[0], CHUNK):
        rows = slice(start, start + CHUNK)
        total = None
        for tile in range(tiles):
            e = e_ref[rows, tile * LANES : (tile + 1) * LANES]
            term = e * e * scale[tile : tile + 1, :]
            total = term if total is None else total + term
        part_ref[rows, :] = total


def cols_first_body(clips, e_ref, in_ref, part_ref, own_total_ref):
    tiles = e_ref.shape[1] // LANES
    size = tiles + 1
    total = in_ref[:size]
    for layer in range(1, in_ref.shape[0] // size):
        total = total + in_ref[layer * size : (layer + 1) * size]
    own_total_ref[...] = jnp.broadcast_to(total[tiles:], (8, LANES))
    weigh_columns(e_ref, 1.0 / (clips * total[:tiles]), part_ref)


def rows_second_body(protos, e_ref, own_ref, other_ref, own_total_ref, out_ref):
    tiles = e_ref.shape[1] // LANES
    masses = masses_of(e_ref, column_scale(own_ref, other_ref, e_ref.shape[0], protos))
    for block in range(tiles):
        out_ref[block, :tiles] = masses
        out_ref[block, tiles:] = own_total_ref[...]


def spread_second_body(in_ref, out_ref, totals_ref):
    tiles = in_ref.shape[0]
    masses = jnp.sum(in_ref[:, :tiles, :], axis=0)
    for layer in range(out_ref.shape[0] // tiles):
        out_ref[layer * tiles : (layer + 1) * tiles] = masses
    for block in range(tiles):
        totals_ref[block : block + 1, :] = in_ref[block, tiles : tiles + 1, :]


def summed_lines(in_ref, size):
    total = in_ref[:size]
    for layer in range(1, in_ref.shape[0] // size):
        total = total + in_ref[layer * size : (layer + 1) * size]
    return total


def cols_second_body(clips, e_ref, in_ref, part_ref):
    weigh_columns(e_ref, 1.0 / (clips * summed_lines(in_ref, e_ref.shape[1] // LANES)), part_ref)


def mates_rows_body(protos, side, spot_ref, first_ref, second_ref, own_ref, other_ref, protos_ref, x_ref, out_ref, scale_ref):
    size = out_ref.shape[0] // side
    pair = 2 * LANES
    scale = column_scale(own_ref, other_ref, protos_ref.shape[0], protos)
    scale_ref[...] = scale
    wide = jnp.concatenate([scale, scale], axis=1)
    turned = turned_protos(protos_ref)
    masses = []
    blocks = first_ref.shape[1] // PAIR
    for block in range(2 * blocks):
        mate_e_ref = first_ref if block < blocks else second_ref
        start = block % blocks * PAIR
        e = mate_e_ref[:, start : start + PAIR]
        kernel = e * e * wide
        mass = jnp.sum(kernel, axis=0, keepdims=True)
        y = times_protos(turned, kernel)
        for half in range(2):
            lanes = slice(half * LANES, (half + 1) * LANES)
            masses.append(mass[:, lanes])
            chip_y, chip_x = divmod(2 * block + half, side)
            along_x, along_y = chip_x * size + chip_y * pair, chip_y * size + chip_x * pair
            start = pl.multiple_of(along_x + spot_ref[2] * (along_y - along_x), 8)
            out_ref[pl.ds(start, LANES), :] = x_ref[2 * block + half]
            out_ref[pl.ds(start + LANES, LANES), :] = y[:, lanes]
    masses = jnp.concatenate(masses, axis=0)
    for block in range(side):
        out_ref[block * size + side * pair : (block + 1) * size] = masses


def cross_body(in_ref, out_ref):
    side = out_ref.shape[0]
    pair = 2 * LANES
    total = jnp.sum(in_ref[...], axis=0)
    for block in range(side):
        out_ref[block, :pair] = total[block * pair : (block + 1) * pair]
        out_ref[block, pair:] = total[side * pair :]


def turn_body(in_ref, out_ref):
    total = jnp.sum(in_ref[...], axis=0)
    x, y, masses = total[:LANES].T, total[LANES : 2 * LANES].T, total[2 * LANES :]
    size = 16 + masses.shape[0]
    for layer in range(out_ref.shape[0] // size):
        base = layer * size
        out_ref[base : base + 8] = x[layer * 8 : layer * 8 + 8]
        out_ref[base + 8 : base + 16] = y[layer * 8 : layer * 8 + 8]
        out_ref[base + 16 : base + size] = masses


def proto_grads(rows, e_ref, first_ref, second_ref, scale_ref, shares, masses, clips_ref):
    scale = scale_ref[rows, :]
    blocks = first_ref.shape[1] // PAIR
    acc = None
    for block in range(2 * blocks):
        mate_e_ref = first_ref if block < blocks else second_ref
        pieces = []
        for half in range(2):
            tile = 2 * block + half
            mate = mate_e_ref[rows, (block % blocks * 2 + half) * LANES : (block % blocks * 2 + half + 1) * LANES]
            e = e_ref[rows, tile * LANES : (tile + 1) * LANES]
            pieces.append(e * shares[tile : tile + 1, :] - mate * mate * scale * masses[tile : tile + 1, :])
        high, low = split(jnp.concatenate(pieces, axis=1))
        clip_high, clip_low = split(clips_ref[block * PAIR : (block + 1) * PAIR, :])
        term = dot(high, jnp.concatenate([clip_high, clip_low], axis=1))
        term = term[:, :LANES] + term[:, LANES:] + dot(low, clip_high)
        acc = term if acc is None else acc + term
    return acc * 10.0


def other_grads_body(e_ref, first_ref, second_ref, scale_ref, totals_ref, in_ref, clips_ref, out_ref, sums_ref, inverse_ref):
    n_rows = out_ref.shape[0]
    tiles = totals_ref.shape[0]
    total = summed_lines(in_ref, 16 + tiles)
    sums_ref[...] = total[:16]
    masses = 1.0 / total[16:]
    shares = 1.0 / totals_ref[...]
    inverse_ref[:tiles] = masses
    inverse_ref[tiles:] = shares
    rows = slice(n_rows, 2 * n_rows)
    out_ref[...] = proto_grads(rows, e_ref, first_ref, second_ref, scale_ref, shares, masses, clips_ref)


def own_values(ref, row, layer):
    values = jnp.broadcast_to(ref[pl.ds(row, 1), :], (8, LANES))
    lane = lax.broadcasted_iota(jnp.int32, (8, LANES), 1)
    line = lax.broadcasted_iota(jnp.int32, (8, LANES), 0)
    return jnp.sum(jnp.where(lane == layer * 8 + line, values, 0.0), axis=1, keepdims=True)


def own_grads_body(e_ref, first_ref, second_ref, scale_ref, inverse_ref, clips_ref, out_ref):
    tiles = inverse_ref.shape[0] // 2
    rows = slice(0, out_ref.shape[0])
    out_ref[...] = proto_grads(
        rows, e_ref, first_ref, second_ref, scale_ref, inverse_ref[tiles:], inverse_ref[:tiles], clips_ref
    )


def finish_body(spot_ref, inverse_ref, sums_ref, embeddings_ref, protos_ref, own_ref, other_ref, clip_ref, proto_ref):
    tiles = inverse_ref.shape[0] // 2
    own_mass = own_values(inverse_ref, spot_ref[0], spot_ref[1])
    own_share = own_values(inverse_ref, spot_ref[0] + tiles, spot_ref[1])
    clip_ref[...] = finish_rows(embeddings_ref[...], 10.0 * (sums_ref[:8] * own_share - sums_ref[8:] * own_mass))
    proto_ref[...] = finish_rows(protos_ref[...], own_ref[...] + other_ref[...])


def local(embeddings, prototypes, partner):
    n_batch, n_proto = lax.axis_size("batch"), lax.axis_size("proto")
    tiles = n_proto // 2
    rows, features = embeddings.shape
    own_protos = prototypes.shape[0]
    clips, protos = float(rows * n_batch * n_proto), float(own_protos * n_batch * n_proto)
    here, n_here = tiles * LANES, 2 * own_protos
    where = lax.axis_index("proto")
    same_core = [[2 * i + c for i in range(tiles)] for c in range(2)]
    side = int(tiles**0.5)
    rows_x = [[[2 * (side * y + x) + c for x in range(side)] for y in range(side)] for c in range(2)]
    rows_y = [[[2 * (side * y + x) + c for y in range(side)] for x in range(side)] for c in range(2)]
    cores = [(i, i ^ 1) for i in range(n_proto)]
    smem = pl.BlockSpec(memory_space=pltpu.SMEM)
    vmem = pl.BlockSpec(memory_space=pltpu.VMEM)

    def swap(values):
        return lax.ppermute(values, "proto", cores)

    def over_chips(blocks):
        return lax.all_to_all(blocks, "proto", 0, 0, tiled=True, axis_index_groups=same_core)

    def over_ring(blocks, groups):
        return lax.all_to_all(blocks, "proto", 0, 0, tiled=True, axis_index_groups=groups)

    def over_layers(lines):
        blocks = lax.all_to_all(lines.reshape(n_batch, 1, -1), "batch", 0, 0, tiled=True)
        return blocks.reshape(lines.shape)

    spot = jnp.stack([where >> 1, lax.axis_index("batch"), where & 1])
    partner = partner.reshape(-1, LANES)
    raw = jnp.concatenate([embeddings, partner.astype(jnp.float32)], axis=0)
    sent = call(functools.partial(send_body, n_proto, rows), f32(n_batch * raw.shape[0], LANES))(raw)
    sent, held, spot = lax.optimization_barrier((sent, prototypes, spot))
    column = over_layers(sent)
    own_units = call(units_body, f32(own_protos, features))(held)
    unit_protos = jnp.concatenate([own_units, swap(own_units)], axis=0)
    column, unit_protos = lax.optimization_barrier((column, unit_protos))
    blocks, places = call(
        column_body,
        (f32(tiles, LANES, features), jax.ShapeDtypeStruct((n_batch, partner.shape[0], LANES), jnp.int32)),
        in_specs=[smem, vmem],
    )(spot, column)
    own_clips = over_chips(blocks).reshape(here, features)

    e, totals, bundle = call(
        scores_body, (f32(n_here, here), f32(tiles, LANES), f32(n_here + here, features))
    )(unit_protos, own_clips)
    x = call(pulls_body, f32(tiles, features, LANES))(unit_protos, e)
    received, x = lax.optimization_barrier((swap(bundle), x))
    blocks = call(functools.partial(rows_first_body, protos), f32(tiles, tiles + 8, LANES))(e, bundle, received, totals)
    lines = call(spread_first_body, f32(n_batch * (tiles + 1), LANES))(over_chips(blocks))
    part, own_total = call(functools.partial(cols_first_body, clips), (f32(n_here, LANES), f32(8, LANES)))(
        e, over_layers(lines)
    )

    mates = pltpu.VMEM((2, PAIR, features), jnp.float32)
    part, late = lax.optimization_barrier((part, places.reshape(-1)))
    first_e, table = call(
        mates_first_body,
        (f32(n_here, here // 2), f32(2 * here, features)),
        in_specs=[smem, smem, vmem, vmem, vmem],
        scratch_shapes=[mates],
    )(late, spot, unit_protos, own_clips, received)
    other, first_e = lax.optimization_barrier((swap(part), first_e))
    blocks = call(functools.partial(rows_second_body, protos), f32(tiles, tiles + 8, LANES))(e, part, other, own_total)
    lines, totals = call(spread_second_body, (f32(n_batch * tiles, LANES), f32(tiles, LANES)))(over_chips(blocks))
    part = call(functools.partial(cols_second_body, clips), f32(n_here, LANES))(e, over_layers(lines))
    part, late = lax.optimization_barrier((part, late))
    second_e = call(
        mates_second_body, f32(n_here, here // 2), in_specs=[smem, smem, vmem, vmem], scratch_shapes=[mates]
    )(late, spot, unit_protos, table)
    other, second_e = lax.optimization_barrier((swap(part), second_e))
    size = side * 2 * features + tiles
    lines, scale = call(
        functools.partial(mates_rows_body, protos, side),
        (f32(side * size, LANES), f32(n_here, LANES)),
        in_specs=[smem] + [vmem] * 6,
    )(spot, first_e, second_e, part, other, unit_protos, x)
    blocks = over_ring(lines.reshape(side, size, LANES), rows_x[0] + rows_y[1])
    blocks = call(cross_body, f32(side, 2 * features + tiles, LANES))(blocks)
    blocks = over_ring(blocks, rows_y[0] + rows_x[1])
    lines = call(turn_body, f32(n_batch * (2 * rows + tiles), LANES))(blocks)
    other_grads, sums, inverse = call(
        other_grads_body, (f32(own_protos, features), f32(2 * rows, features), f32(2 * tiles, LANES))
    )(e, first_e, second_e, scale, totals, over_layers(lines), own_clips)
    own_grads = call(own_grads_body, f32(own_protos, features))(e, first_e, second_e, scale, inverse, own_clips)
    return call(
        finish_body, (f32(rows, features), f32(own_protos, features)), in_specs=[smem] + [vmem] * 6
    )(spot, inverse, sums, embeddings, prototypes, own_grads, swap(other_grads))


def solution(mesh):
    in_specs = (P(("batch", "proto"), None), P(("batch", "proto"), None), P("batch"))
    out_specs = (P(("batch", "proto"), None), P(("batch", "proto"), None))
    return jax.shard_map(local, mesh=mesh, in_specs=in_specs, out_specs=out_specs, check_vma=False)
```

```python
import functools

import jax
import jax.numpy as jnp
from jax import lax
from jax.experimental import pallas as pl
from jax.experimental.pallas import tpu as pltpu
from jax.sharding import PartitionSpec as P

LANES = 128
PAIR = 2 * LANES
CHUNK = 64
VMEM_BYTES = 24 * 1024 * 1024


def inverse_norms(values):
    return 1.0 / jnp.sqrt(jnp.sum(values * values, axis=1, keepdims=True) + 1e-06)


def finish_rows(values, grads):
    inverse = inverse_norms(values)
    units = values * inverse
    return inverse * (grads - units * jnp.sum(units * grads, axis=1, keepdims=True))


def split(values):
    high = values.astype(jnp.bfloat16)
    low = (values - high.astype(jnp.float32)).astype(jnp.bfloat16)
    return high, low


def dot(left, right):
    return jnp.dot(left, right, preferred_element_type=jnp.float32)


def dot_rows(left, right):
    return lax.dot_general(left, right, (((1,), (1,)), ((), ())), preferred_element_type=jnp.float32)


def call(body, out_shape, **kwargs):
    return pl.pallas_call(
        body, out_shape=out_shape, compiler_params=pltpu.CompilerParams(vmem_limit_bytes=VMEM_BYTES), **kwargs
    )


def f32(*shape):
    return jax.ShapeDtypeStruct(shape, jnp.float32)


def exponents(proto_pair, clips):
    high, low = split(clips)
    scores = dot_rows(proto_pair, jnp.concatenate([high, high], axis=1))
    scores = scores + dot_rows(proto_pair, jnp.concatenate([low, low], axis=1))
    return jnp.exp(scores * 10.0)


def scores_body(protos_ref, clips_ref, e_ref, total_ref, bundle_ref):
    n_here = protos_ref.shape[0]
    pair = jnp.concatenate(split(protos_ref[...]), axis=1)
    for block in range(clips_ref.shape[0] // PAIR):
        cols = slice(block * PAIR, (block + 1) * PAIR)
        clips = clips_ref[cols, :]
        bundle_ref[n_here + block * PAIR : n_here + (block + 1) * PAIR] = clips
        e = exponents(pair, clips)
        e_ref[:, cols] = e
        kernel = e * e
        both = kernel[:, :LANES] + kernel[:, LANES:]
        bundle_ref[:n_here] = both if block == 0 else bundle_ref[:n_here] + both
        totals = jnp.sum(e, axis=0, keepdims=True)
        for half in range(2):
            total_ref[2 * block + half : 2 * block + half + 1, :] = totals[:, half * LANES : (half + 1) * LANES]


def turned_protos(protos_ref):
    high, low = split(protos_ref[...].T)
    return jnp.concatenate([high, low], axis=0)


def times_protos(turned, weights):
    high, low = split(weights)
    both = dot(turned, high)
    return both[:LANES] + both[LANES:] + dot(turned[:LANES], low)


def ring_start(tile, side, size):
    return tile // side * size + tile % side * 2 * LANES


def pulls_body(side, protos_ref, e_ref, out_ref):
    turned = turned_protos(protos_ref)
    size = out_ref.shape[0] // side
    for block in range(e_ref.shape[1] // PAIR):
        x = times_protos(turned, e_ref[:, block * PAIR : (block + 1) * PAIR])
        for half in range(2):
            start = ring_start(2 * block + half, side, size)
            out_ref[start : start + LANES] = x[:, half * LANES : (half + 1) * LANES]


def mates_of(part, index_ref, spot_ref, protos_ref, table_ref, e_ref, mate_ref):
    pair = jnp.concatenate(split(protos_ref[...]), axis=1)
    blocks = e_ref.shape[1] // PAIR
    tiles = 4 * blocks
    core, side = spot_ref[2], int(tiles**0.5)
    for block in range(blocks):
        slot = block % 2
        for half in range(2):
            tile = 2 * (part * blocks + block) + half
            crossed = tile % side * side + tile // side
            first = crossed * 16 + core * ((tile - crossed) * 16 + 8)
            for z in range(LANES // 8):
                start = first + z * tiles * 16
                for r in range(8):
                    row = half * LANES + z * 8 + r
                    mate_ref[slot, row : row + 1, :] = table_ref[pl.ds(index_ref[start + r], 1), :]
        e_ref[:, block * PAIR : (block + 1) * PAIR] = exponents(pair, mate_ref[slot])


def mates_first_body(index_ref, spot_ref, protos_ref, own_ref, other_ref, e_ref, table_ref, mate_ref):
    rows = own_ref.shape[0]
    table_ref[:rows] = own_ref[...]
    table_ref[rows:] = other_ref[protos_ref.shape[0] :]
    mates_of(0, index_ref, spot_ref, protos_ref, table_ref, e_ref, mate_ref)


def mates_second_body(index_ref, spot_ref, protos_ref, table_ref, e_ref, mate_ref):
    mates_of(1, index_ref, spot_ref, protos_ref, table_ref, e_ref, mate_ref)


def column_scale(own_ref, other_ref, rows, protos):
    half = rows // 2
    part = jnp.concatenate([own_ref[:half] + other_ref[half:rows], own_ref[half:rows] + other_ref[:half]], axis=0)
    scale = 1.0 / (protos * jnp.sum(part, axis=1, keepdims=True))
    return jnp.broadcast_to(scale, (rows, LANES))


def row_mass(e_ref, scale, tile):
    e = e_ref[:, tile * LANES : (tile + 1) * LANES]
    return jnp.sum(e * e * scale, axis=0, keepdims=True)


def units_body(in_ref, out_ref):
    values = in_ref[...]
    out_ref[...] = values * inverse_norms(values)


def send_body(n_proto, rows, in_ref, out_ref):
    values = in_ref[:rows]
    partner = in_ref[rows:].astype(jnp.int32)
    line = partner & (rows - 1)
    slot = (partner // rows) & (n_proto - 1)
    side = int((n_proto // 2) ** 0.5)
    chip, core = slot >> 1, slot & 1
    tile = jnp.where(core > 0, chip, (chip & (side - 1)) * side + chip // side)
    place = core * (n_proto // 2) + tile
    place = place * LANES + partner // (rows * n_proto) * rows + line
    block = jnp.concatenate([values * inverse_norms(values), place.astype(jnp.float32)], axis=0)
    for layer in range(out_ref.shape[0] // block.shape[0]):
        out_ref[layer * block.shape[0] : (layer + 1) * block.shape[0]] = block


def column_body(spot_ref, in_ref, out_ref, places_ref):
    per_layer = places_ref.shape[1]
    size = 8 + per_layer
    places = []
    for layer in range(places_ref.shape[0]):
        units = in_ref[layer * size : layer * size + 8]
        places.append(in_ref[layer * size + 8 : (layer + 1) * size][None])
        for block in range(out_ref.shape[0]):
            out_ref[block, layer * 8 : layer * 8 + 8] = units
    here = out_ref.shape[0] * LANES
    places = jnp.concatenate(places, axis=0).astype(jnp.int32)
    moved = jnp.where(places >= here, places - here, places + here)
    places_ref[...] = jnp.where(spot_ref[2] > 0, moved, places)


def masses_of(e_ref, scale):
    tiles = e_ref.shape[1] // LANES
    return jnp.concatenate([row_mass(e_ref, scale, tile) for tile in range(tiles)], axis=0)


def rows_first_body(protos, e_ref, own_ref, other_ref, totals_ref, out_ref):
    tiles = e_ref.shape[1] // LANES
    scale = column_scale(own_ref, other_ref, e_ref.shape[0], protos)
    masses = masses_of(e_ref, scale)
    for block in range(tiles):
        out_ref[block, :tiles] = masses
        out_ref[block, tiles:] = jnp.broadcast_to(totals_ref[block : block + 1, :], (8, LANES))


def spread_first_body(in_ref, out_ref):
    tiles = in_ref.shape[0]
    total = jnp.sum(in_ref[...], axis=0)
    size = tiles + 1
    for layer in range(out_ref.shape[0] // size):
        out_ref[layer * size : (layer + 1) * size] = total[:size]


def weigh_columns(e_ref, scale, part_ref):
    tiles = e_ref.shape[1] // LANES
    for start in range(0, e_ref.shape[0], CHUNK):
        rows = slice(start, start + CHUNK)
        total = None
        for tile in range(tiles):
            e = e_ref[rows, tile * LANES : (tile + 1) * LANES]
            term = e * e * scale[tile : tile + 1, :]
            total = term if total is None else total + term
        part_ref[rows, :] = total


def cols_first_body(clips, e_ref, in_ref, part_ref, own_total_ref):
    tiles = e_ref.shape[1] // LANES
    size = tiles + 1
    total = in_ref[:size]
    for layer in range(1, in_ref.shape[0] // size):
        total = total + in_ref[layer * size : (layer + 1) * size]
    own_total_ref[...] = jnp.broadcast_to(total[tiles:], (8, LANES))
    weigh_columns(e_ref, 1.0 / (clips * total[:tiles]), part_ref)


def rows_second_body(protos, e_ref, own_ref, other_ref, own_total_ref, out_ref):
    tiles = e_ref.shape[1] // LANES
    masses = masses_of(e_ref, column_scale(own_ref, other_ref, e_ref.shape[0], protos))
    for block in range(tiles):
        out_ref[block, :tiles] = masses
        out_ref[block, tiles:] = own_total_ref[...]


def spread_second_body(in_ref, out_ref, totals_ref):
    tiles = in_ref.shape[0]
    masses = jnp.sum(in_ref[:, :tiles, :], axis=0)
    for layer in range(out_ref.shape[0] // tiles):
        out_ref[layer * tiles : (layer + 1) * tiles] = masses
    for block in range(tiles):
        totals_ref[block : block + 1, :] = in_ref[block, tiles : tiles + 1, :]


def summed_lines(in_ref, size):
    total = in_ref[:size]
    for layer in range(1, in_ref.shape[0] // size):
        total = total + in_ref[layer * size : (layer + 1) * size]
    return total


def cols_second_body(clips, e_ref, in_ref, part_ref):
    weigh_columns(e_ref, 1.0 / (clips * summed_lines(in_ref, e_ref.shape[1] // LANES)), part_ref)


def mates_rows_body(protos, side, first_ref, second_ref, own_ref, other_ref, protos_ref, _, out_ref, scale_ref):
    size = out_ref.shape[0] // side
    pair = 2 * LANES
    scale = column_scale(own_ref, other_ref, protos_ref.shape[0], protos)
    scale_ref[...] = scale
    wide = jnp.concatenate([scale, scale], axis=1)
    turned = turned_protos(protos_ref)
    masses = []
    blocks = first_ref.shape[1] // PAIR
    for block in range(2 * blocks):
        mate_e_ref = first_ref if block < blocks else second_ref
        start = block % blocks * PAIR
        e = mate_e_ref[:, start : start + PAIR]
        kernel = e * e * wide
        mass = jnp.sum(kernel, axis=0, keepdims=True)
        y = times_protos(turned, kernel)
        for half in range(2):
            lanes = slice(half * LANES, (half + 1) * LANES)
            masses.append(mass[:, lanes])
            start = ring_start(2 * block + half, side, size) + LANES
            out_ref[start : start + LANES] = y[:, lanes]
    masses = jnp.concatenate(masses, axis=0)
    for block in range(side):
        out_ref[block * size + side * pair : (block + 1) * size] = masses


def cross_body(in_ref, out_ref):
    side = out_ref.shape[0]
    pair = 2 * LANES
    total = jnp.sum(in_ref[...], axis=0)
    for block in range(side):
        out_ref[block, :pair] = total[block * pair : (block + 1) * pair]
        out_ref[block, pair:] = total[side * pair :]


def turn_body(in_ref, out_ref):
    total = jnp.sum(in_ref[...], axis=0)
    x, y, masses = total[:LANES].T, total[LANES : 2 * LANES].T, total[2 * LANES :]
    size = 16 + masses.shape[0]
    for layer in range(out_ref.shape[0] // size):
        base = layer * size
        out_ref[base : base + 8] = x[layer * 8 : layer * 8 + 8]
        out_ref[base + 8 : base + 16] = y[layer * 8 : layer * 8 + 8]
        out_ref[base + 16 : base + size] = masses


def proto_grads(rows, e_ref, first_ref, second_ref, scale_ref, shares, masses, clips_ref):
    scale = scale_ref[rows, :]
    blocks = first_ref.shape[1] // PAIR
    acc = None
    for block in range(2 * blocks):
        mate_e_ref = first_ref if block < blocks else second_ref
        pieces = []
        for half in range(2):
            tile = 2 * block + half
            mate = mate_e_ref[rows, (block % blocks * 2 + half) * LANES : (block % blocks * 2 + half + 1) * LANES]
            e = e_ref[rows, tile * LANES : (tile + 1) * LANES]
            pieces.append(e * shares[tile : tile + 1, :] - mate * mate * scale * masses[tile : tile + 1, :])
        high, low = split(jnp.concatenate(pieces, axis=1))
        clip_high, clip_low = split(clips_ref[block * PAIR : (block + 1) * PAIR, :])
        term = dot(high, jnp.concatenate([clip_high, clip_low], axis=1))
        term = term[:, :LANES] + term[:, LANES:] + dot(low, clip_high)
        acc = term if acc is None else acc + term
    return acc * 10.0


def other_grads_body(e_ref, first_ref, second_ref, scale_ref, totals_ref, in_ref, clips_ref, out_ref, sums_ref, inverse_ref):
    n_rows = out_ref.shape[0]
    tiles = totals_ref.shape[0]
    total = summed_lines(in_ref, 16 + tiles)
    sums_ref[...] = total[:16]
    masses = 1.0 / total[16:]
    shares = 1.0 / totals_ref[...]
    inverse_ref[:tiles] = masses
    inverse_ref[tiles:] = shares
    rows = slice(n_rows, 2 * n_rows)
    out_ref[...] = proto_grads(rows, e_ref, first_ref, second_ref, scale_ref, shares, masses, clips_ref)


def own_values(ref, row, layer):
    values = jnp.broadcast_to(ref[pl.ds(row, 1), :], (8, LANES))
    lane = lax.broadcasted_iota(jnp.int32, (8, LANES), 1)
    line = lax.broadcasted_iota(jnp.int32, (8, LANES), 0)
    return jnp.sum(jnp.where(lane == layer * 8 + line, values, 0.0), axis=1, keepdims=True)


def own_grads_body(e_ref, first_ref, second_ref, scale_ref, inverse_ref, clips_ref, out_ref):
    tiles = inverse_ref.shape[0] // 2
    rows = slice(0, out_ref.shape[0])
    out_ref[...] = proto_grads(
        rows, e_ref, first_ref, second_ref, scale_ref, inverse_ref[tiles:], inverse_ref[:tiles], clips_ref
    )


def finish_body(spot_ref, inverse_ref, sums_ref, embeddings_ref, protos_ref, own_ref, other_ref, clip_ref, proto_ref):
    tiles = inverse_ref.shape[0] // 2
    own_mass = own_values(inverse_ref, spot_ref[0], spot_ref[1])
    own_share = own_values(inverse_ref, spot_ref[0] + tiles, spot_ref[1])
    clip_ref[...] = finish_rows(embeddings_ref[...], 10.0 * (sums_ref[:8] * own_share - sums_ref[8:] * own_mass))
    proto_ref[...] = finish_rows(protos_ref[...], own_ref[...] + other_ref[...])


def local(embeddings, prototypes, partner):
    n_batch, n_proto = lax.axis_size("batch"), lax.axis_size("proto")
    tiles = n_proto // 2
    rows, features = embeddings.shape
    own_protos = prototypes.shape[0]
    clips, protos = float(rows * n_batch * n_proto), float(own_protos * n_batch * n_proto)
    here, n_here = tiles * LANES, 2 * own_protos
    where = lax.axis_index("proto")
    side = int(tiles**0.5)
    crossed = [tile % side * side + tile // side for tile in range(tiles)]
    same_core = [[2 * chip for chip in crossed], [2 * chip + 1 for chip in range(tiles)]]
    rows_x = [[[2 * (side * y + x) + c for x in range(side)] for y in range(side)] for c in range(2)]
    rows_y = [[[2 * (side * y + x) + c for y in range(side)] for x in range(side)] for c in range(2)]
    cores = [(i, i ^ 1) for i in range(n_proto)]
    smem = pl.BlockSpec(memory_space=pltpu.SMEM)
    vmem = pl.BlockSpec(memory_space=pltpu.VMEM)

    def swap(values):
        return lax.ppermute(values, "proto", cores)

    def over_chips(blocks):
        return lax.all_to_all(blocks, "proto", 0, 0, tiled=True, axis_index_groups=same_core)

    def over_ring(blocks, groups):
        return lax.all_to_all(blocks, "proto", 0, 0, tiled=True, axis_index_groups=groups)

    def over_layers(lines):
        blocks = lax.all_to_all(lines.reshape(n_batch, 1, -1), "batch", 0, 0, tiled=True)
        return blocks.reshape(lines.shape)

    chip, core = where >> 1, where & 1
    tile = jnp.where(core > 0, chip, chip % side * side + chip // side)
    spot = jnp.stack([tile, lax.axis_index("batch"), core])
    partner = partner.reshape(-1, LANES)
    raw = jnp.concatenate([embeddings, partner.astype(jnp.float32)], axis=0)
    sent = call(functools.partial(send_body, n_proto, rows), f32(n_batch * raw.shape[0], LANES))(raw)
    sent, held, spot = lax.optimization_barrier((sent, prototypes, spot))
    column = over_layers(sent)
    own_units = call(units_body, f32(own_protos, features))(held)
    unit_protos = jnp.concatenate([own_units, swap(own_units)], axis=0)
    column, unit_protos = lax.optimization_barrier((column, unit_protos))
    blocks, places = call(
        column_body,
        (f32(tiles, LANES, features), jax.ShapeDtypeStruct((n_batch, partner.shape[0], LANES), jnp.int32)),
        in_specs=[smem, vmem],
    )(spot, column)
    own_clips = over_chips(blocks).reshape(here, features)

    e, totals, bundle = call(
        scores_body, (f32(n_here, here), f32(tiles, LANES), f32(n_here + here, features))
    )(unit_protos, own_clips)
    size = side * 2 * features + tiles
    pulls = call(functools.partial(pulls_body, side), f32(side * size, LANES))(unit_protos, e)
    received, pulls = lax.optimization_barrier((swap(bundle), pulls))
    blocks = call(functools.partial(rows_first_body, protos), f32(tiles, tiles + 8, LANES))(e, bundle, received, totals)
    lines = call(spread_first_body, f32(n_batch * (tiles + 1), LANES))(over_chips(blocks))
    part, own_total = call(functools.partial(cols_first_body, clips), (f32(n_here, LANES), f32(8, LANES)))(
        e, over_layers(lines)
    )

    mates = pltpu.VMEM((2, PAIR, features), jnp.float32)
    part, late = lax.optimization_barrier((part, places.reshape(-1)))
    first_e, table = call(
        mates_first_body,
        (f32(n_here, here // 2), f32(2 * here, features)),
        in_specs=[smem, smem, vmem, vmem, vmem],
        scratch_shapes=[mates],
    )(late, spot, unit_protos, own_clips, received)
    other, first_e = lax.optimization_barrier((swap(part), first_e))
    blocks = call(functools.partial(rows_second_body, protos), f32(tiles, tiles + 8, LANES))(e, part, other, own_total)
    lines, totals = call(spread_second_body, (f32(n_batch * tiles, LANES), f32(tiles, LANES)))(over_chips(blocks))
    part = call(functools.partial(cols_second_body, clips), f32(n_here, LANES))(e, over_layers(lines))
    part, late = lax.optimization_barrier((part, late))
    second_e = call(
        mates_second_body, f32(n_here, here // 2), in_specs=[smem, smem, vmem, vmem], scratch_shapes=[mates]
    )(late, spot, unit_protos, table)
    other, second_e = lax.optimization_barrier((swap(part), second_e))
    lines, scale = call(
        functools.partial(mates_rows_body, protos, side),
        (f32(side * size, LANES), f32(n_here, LANES)),
        input_output_aliases={5: 0},
    )(first_e, second_e, part, other, unit_protos, pulls)
    blocks = over_ring(lines.reshape(side, size, LANES), rows_x[0] + rows_y[1])
    blocks = call(cross_body, f32(side, 2 * features + tiles, LANES))(blocks)
    blocks = over_ring(blocks, rows_y[0] + rows_x[1])
    lines = call(turn_body, f32(n_batch * (2 * rows + tiles), LANES))(blocks)
    other_grads, sums, inverse = call(
        other_grads_body, (f32(own_protos, features), f32(2 * rows, features), f32(2 * tiles, LANES))
    )(e, first_e, second_e, scale, totals, over_layers(lines), own_clips)
    own_grads = call(own_grads_body, f32(own_protos, features))(e, first_e, second_e, scale, inverse, own_clips)
    return call(
        finish_body, (f32(rows, features), f32(own_protos, features)), in_specs=[smem] + [vmem] * 6
    )(spot, inverse, sums, embeddings, prototypes, own_grads, swap(other_grads))


def solution(mesh):
    in_specs = (P(("batch", "proto"), None), P(("batch", "proto"), None), P("batch"))
    out_specs = (P(("batch", "proto"), None), P(("batch", "proto"), None))
    return jax.shard_map(local, mesh=mesh, in_specs=in_specs, out_specs=out_specs, check_vma=False)
```

```python
import functools

import jax
import jax.numpy as jnp
from jax import lax
from jax.experimental import pallas as pl
from jax.experimental.pallas import tpu as pltpu
from jax.sharding import PartitionSpec as P

LANES = 128
PAIR = 2 * LANES
CHUNK = 64
VMEM_BYTES = 24 * 1024 * 1024


def inverse_norms(values):
    return 1.0 / jnp.sqrt(jnp.sum(values * values, axis=1, keepdims=True) + 1e-06)


def finish_rows(values, grads):
    inverse = inverse_norms(values)
    units = values * inverse
    return inverse * (grads - units * jnp.sum(units * grads, axis=1, keepdims=True))


def split(values):
    high = values.astype(jnp.bfloat16)
    low = (values - high.astype(jnp.float32)).astype(jnp.bfloat16)
    return high, low


def dot(left, right):
    return jnp.dot(left, right, preferred_element_type=jnp.float32)


def dot_rows(left, right):
    return lax.dot_general(left, right, (((1,), (1,)), ((), ())), preferred_element_type=jnp.float32)


def call(body, out_shape, **kwargs):
    return pl.pallas_call(
        body, out_shape=out_shape, compiler_params=pltpu.CompilerParams(vmem_limit_bytes=VMEM_BYTES), **kwargs
    )


def f32(*shape):
    return jax.ShapeDtypeStruct(shape, jnp.float32)


def exponents(proto_pair, clips):
    high, low = split(clips)
    scores = dot_rows(proto_pair, jnp.concatenate([high, high], axis=1))
    scores = scores + dot_rows(proto_pair, jnp.concatenate([low, low], axis=1))
    return jnp.exp(scores * 10.0)


def scores_body(protos_ref, clips_ref, e_ref, total_ref, bundle_ref):
    n_here = protos_ref.shape[0]
    pair = jnp.concatenate(split(protos_ref[...]), axis=1)
    for block in range(clips_ref.shape[0] // PAIR):
        cols = slice(block * PAIR, (block + 1) * PAIR)
        clips = clips_ref[cols, :]
        bundle_ref[n_here + block * PAIR : n_here + (block + 1) * PAIR] = clips
        e = exponents(pair, clips)
        e_ref[:, cols] = e
        kernel = e * e
        both = kernel[:, :LANES] + kernel[:, LANES:]
        bundle_ref[:n_here] = both if block == 0 else bundle_ref[:n_here] + both
        totals = jnp.sum(e, axis=0, keepdims=True)
        for half in range(2):
            total_ref[2 * block + half : 2 * block + half + 1, :] = totals[:, half * LANES : (half + 1) * LANES]


def turned_protos(protos_ref):
    high, low = split(protos_ref[...].T)
    return jnp.concatenate([high, low], axis=0)


def times_protos(turned, weights):
    high, low = split(weights)
    both = dot(turned, high)
    return both[:LANES] + both[LANES:] + dot(turned[:LANES], low)


def ring_start(tile, side, size):
    return tile // side * size + tile % side * 2 * LANES


def pulls_body(side, protos_ref, e_ref, clips_ref, out_ref, table_ref):
    table_ref[: clips_ref.shape[0]] = clips_ref[...]
    turned = turned_protos(protos_ref)
    size = out_ref.shape[0] // side
    for block in range(e_ref.shape[1] // PAIR):
        x = times_protos(turned, e_ref[:, block * PAIR : (block + 1) * PAIR])
        for half in range(2):
            start = ring_start(2 * block + half, side, size)
            out_ref[start : start + LANES] = x[:, half * LANES : (half + 1) * LANES]


def mates_of(part, index_ref, spot_ref, protos_ref, table_ref, e_ref, mate_ref):
    pair = jnp.concatenate(split(protos_ref[...]), axis=1)
    blocks = e_ref.shape[1] // PAIR
    tiles = 4 * blocks
    core, side = spot_ref[2], int(tiles**0.5)
    for block in range(blocks):
        slot = block % 2
        for half in range(2):
            tile = 2 * (part * blocks + block) + half
            crossed = tile % side * side + tile // side
            first = crossed * 16 + core * ((tile - crossed) * 16 + 8)
            for z in range(LANES // 8):
                start = first + z * tiles * 16
                for r in range(8):
                    row = half * LANES + z * 8 + r
                    mate_ref[slot, row : row + 1, :] = table_ref[pl.ds(index_ref[start + r], 1), :]
        e_ref[:, block * PAIR : (block + 1) * PAIR] = exponents(pair, mate_ref[slot])


def mates_first_body(index_ref, spot_ref, protos_ref, other_ref, _, e_ref, table_ref, mate_ref):
    rows = table_ref.shape[0] // 2
    table_ref[rows:] = other_ref[protos_ref.shape[0] :]
    mates_of(0, index_ref, spot_ref, protos_ref, table_ref, e_ref, mate_ref)


def mates_second_body(index_ref, spot_ref, protos_ref, table_ref, e_ref, mate_ref):
    mates_of(1, index_ref, spot_ref, protos_ref, table_ref, e_ref, mate_ref)


def column_scale(own_ref, other_ref, rows, protos):
    half = rows // 2
    part = jnp.concatenate([own_ref[:half] + other_ref[half:rows], own_ref[half:rows] + other_ref[:half]], axis=0)
    scale = 1.0 / (protos * jnp.sum(part, axis=1, keepdims=True))
    return jnp.broadcast_to(scale, (rows, LANES))


def row_mass(e_ref, scale, tile):
    e = e_ref[:, tile * LANES : (tile + 1) * LANES]
    return jnp.sum(e * e * scale, axis=0, keepdims=True)


def units_body(in_ref, out_ref):
    values = in_ref[...]
    out_ref[...] = values * inverse_norms(values)


def send_body(n_proto, rows, in_ref, out_ref):
    values = in_ref[:rows]
    partner = in_ref[rows:].astype(jnp.int32)
    line = partner & (rows - 1)
    slot = (partner // rows) & (n_proto - 1)
    side = int((n_proto // 2) ** 0.5)
    chip, core = slot >> 1, slot & 1
    tile = jnp.where(core > 0, chip, (chip & (side - 1)) * side + chip // side)
    place = core * (n_proto // 2) + tile
    place = place * LANES + partner // (rows * n_proto) * rows + line
    block = jnp.concatenate([values * inverse_norms(values), place.astype(jnp.float32)], axis=0)
    for layer in range(out_ref.shape[0] // block.shape[0]):
        out_ref[layer * block.shape[0] : (layer + 1) * block.shape[0]] = block


def column_body(spot_ref, in_ref, out_ref, places_ref):
    per_layer = places_ref.shape[1]
    size = 8 + per_layer
    places = []
    for layer in range(places_ref.shape[0]):
        units = in_ref[layer * size : layer * size + 8]
        places.append(in_ref[layer * size + 8 : (layer + 1) * size][None])
        for block in range(out_ref.shape[0]):
            out_ref[block, layer * 8 : layer * 8 + 8] = units
    here = out_ref.shape[0] * LANES
    places = jnp.concatenate(places, axis=0).astype(jnp.int32)
    moved = jnp.where(places >= here, places - here, places + here)
    places_ref[...] = jnp.where(spot_ref[2] > 0, moved, places)


def masses_of(e_ref, scale):
    tiles = e_ref.shape[1] // LANES
    return jnp.concatenate([row_mass(e_ref, scale, tile) for tile in range(tiles)], axis=0)


def rows_first_body(protos, e_ref, own_ref, other_ref, totals_ref, out_ref):
    tiles = e_ref.shape[1] // LANES
    scale = column_scale(own_ref, other_ref, e_ref.shape[0], protos)
    masses = masses_of(e_ref, scale)
    for block in range(tiles):
        out_ref[block, :tiles] = masses
        out_ref[block, tiles:] = jnp.broadcast_to(totals_ref[block : block + 1, :], (8, LANES))


def spread_first_body(in_ref, out_ref):
    tiles = in_ref.shape[0]
    total = jnp.sum(in_ref[...], axis=0)
    size = tiles + 1
    for layer in range(out_ref.shape[0] // size):
        out_ref[layer * size : (layer + 1) * size] = total[:size]


def weigh_columns(e_ref, scale, part_ref):
    tiles = e_ref.shape[1] // LANES
    for start in range(0, e_ref.shape[0], CHUNK):
        rows = slice(start, start + CHUNK)
        total = None
        for tile in range(tiles):
            e = e_ref[rows, tile * LANES : (tile + 1) * LANES]
            term = e * e * scale[tile : tile + 1, :]
            total = term if total is None else total + term
        part_ref[rows, :] = total


def cols_first_body(clips, e_ref, in_ref, part_ref, own_total_ref):
    tiles = e_ref.shape[1] // LANES
    size = tiles + 1
    total = in_ref[:size]
    for layer in range(1, in_ref.shape[0] // size):
        total = total + in_ref[layer * size : (layer + 1) * size]
    own_total_ref[...] = jnp.broadcast_to(total[tiles:], (8, LANES))
    weigh_columns(e_ref, 1.0 / (clips * total[:tiles]), part_ref)


def rows_second_body(protos, e_ref, own_ref, other_ref, own_total_ref, out_ref):
    tiles = e_ref.shape[1] // LANES
    masses = masses_of(e_ref, column_scale(own_ref, other_ref, e_ref.shape[0], protos))
    for block in range(tiles):
        out_ref[block, :tiles] = masses
        out_ref[block, tiles:] = own_total_ref[...]


def spread_second_body(in_ref, out_ref, totals_ref):
    tiles = in_ref.shape[0]
    masses = jnp.sum(in_ref[:, :tiles, :], axis=0)
    for layer in range(out_ref.shape[0] // tiles):
        out_ref[layer * tiles : (layer + 1) * tiles] = masses
    for block in range(tiles):
        totals_ref[block : block + 1, :] = in_ref[block, tiles : tiles + 1, :]


def summed_lines(in_ref, size):
    total = in_ref[:size]
    for layer in range(1, in_ref.shape[0] // size):
        total = total + in_ref[layer * size : (layer + 1) * size]
    return total


def cols_second_body(clips, e_ref, in_ref, part_ref):
    weigh_columns(e_ref, 1.0 / (clips * summed_lines(in_ref, e_ref.shape[1] // LANES)), part_ref)


def mates_rows_body(protos, side, first_ref, second_ref, own_ref, other_ref, protos_ref, _, out_ref, scale_ref):
    size = out_ref.shape[0] // side
    pair = 2 * LANES
    scale = column_scale(own_ref, other_ref, protos_ref.shape[0], protos)
    scale_ref[...] = scale
    wide = jnp.concatenate([scale, scale], axis=1)
    turned = turned_protos(protos_ref)
    masses = []
    blocks = first_ref.shape[1] // PAIR
    for block in range(2 * blocks):
        mate_e_ref = first_ref if block < blocks else second_ref
        start = block % blocks * PAIR
        e = mate_e_ref[:, start : start + PAIR]
        kernel = e * e * wide
        mass = jnp.sum(kernel, axis=0, keepdims=True)
        y = times_protos(turned, kernel)
        for half in range(2):
            lanes = slice(half * LANES, (half + 1) * LANES)
            masses.append(mass[:, lanes])
            start = ring_start(2 * block + half, side, size) + LANES
            out_ref[start : start + LANES] = y[:, lanes]
    masses = jnp.concatenate(masses, axis=0)
    for block in range(side):
        out_ref[block * size + side * pair : (block + 1) * size] = masses


def cross_body(in_ref, out_ref):
    side = out_ref.shape[0]
    pair = 2 * LANES
    total = jnp.sum(in_ref[...], axis=0)
    for block in range(side):
        out_ref[block, :pair] = total[block * pair : (block + 1) * pair]
        out_ref[block, pair:] = total[side * pair :]


def turn_body(in_ref, out_ref):
    total = jnp.sum(in_ref[...], axis=0)
    x, y, masses = total[:LANES].T, total[LANES : 2 * LANES].T, total[2 * LANES :]
    size = 16 + masses.shape[0]
    for layer in range(out_ref.shape[0] // size):
        base = layer * size
        out_ref[base : base + 8] = x[layer * 8 : layer * 8 + 8]
        out_ref[base + 8 : base + 16] = y[layer * 8 : layer * 8 + 8]
        out_ref[base + 16 : base + size] = masses


def proto_grads(rows, e_ref, first_ref, second_ref, scale_ref, shares, masses, clips_ref):
    scale = scale_ref[rows, :]
    blocks = first_ref.shape[1] // PAIR
    acc = None
    for block in range(2 * blocks):
        mate_e_ref = first_ref if block < blocks else second_ref
        pieces = []
        for half in range(2):
            tile = 2 * block + half
            mate = mate_e_ref[rows, (block % blocks * 2 + half) * LANES : (block % blocks * 2 + half + 1) * LANES]
            e = e_ref[rows, tile * LANES : (tile + 1) * LANES]
            pieces.append(e * shares[tile : tile + 1, :] - mate * mate * scale * masses[tile : tile + 1, :])
        high, low = split(jnp.concatenate(pieces, axis=1))
        clip_high, clip_low = split(clips_ref[block * PAIR : (block + 1) * PAIR, :])
        term = dot(high, jnp.concatenate([clip_high, clip_low], axis=1))
        term = term[:, :LANES] + term[:, LANES:] + dot(low, clip_high)
        acc = term if acc is None else acc + term
    return acc * 10.0


def other_grads_body(e_ref, first_ref, second_ref, scale_ref, totals_ref, in_ref, clips_ref, out_ref, sums_ref, inverse_ref):
    n_rows = out_ref.shape[0]
    tiles = totals_ref.shape[0]
    total = summed_lines(in_ref, 16 + tiles)
    sums_ref[...] = total[:16]
    masses = 1.0 / total[16:]
    shares = 1.0 / totals_ref[...]
    inverse_ref[:tiles] = masses
    inverse_ref[tiles:] = shares
    rows = slice(n_rows, 2 * n_rows)
    out_ref[...] = proto_grads(rows, e_ref, first_ref, second_ref, scale_ref, shares, masses, clips_ref)


def own_values(ref, row, layer):
    values = jnp.broadcast_to(ref[pl.ds(row, 1), :], (8, LANES))
    lane = lax.broadcasted_iota(jnp.int32, (8, LANES), 1)
    line = lax.broadcasted_iota(jnp.int32, (8, LANES), 0)
    return jnp.sum(jnp.where(lane == layer * 8 + line, values, 0.0), axis=1, keepdims=True)


def own_grads_body(e_ref, first_ref, second_ref, scale_ref, inverse_ref, clips_ref, out_ref):
    tiles = inverse_ref.shape[0] // 2
    rows = slice(0, out_ref.shape[0])
    out_ref[...] = proto_grads(
        rows, e_ref, first_ref, second_ref, scale_ref, inverse_ref[tiles:], inverse_ref[:tiles], clips_ref
    )


def finish_body(spot_ref, inverse_ref, sums_ref, embeddings_ref, protos_ref, own_ref, other_ref, clip_ref, proto_ref,
                clip_held, proto_held, sems):
    copies = [
        pltpu.make_async_copy(proto_held, proto_ref, sems.at[0]),
        pltpu.make_async_copy(clip_held, clip_ref, sems.at[1]),
    ]
    proto_held[...] = finish_rows(protos_ref[...], own_ref[...] + other_ref[...])
    copies[0].start()
    tiles = inverse_ref.shape[0] // 2
    own_mass = own_values(inverse_ref, spot_ref[0], spot_ref[1])
    own_share = own_values(inverse_ref, spot_ref[0] + tiles, spot_ref[1])
    clip_held[...] = finish_rows(embeddings_ref[...], 10.0 * (sums_ref[:8] * own_share - sums_ref[8:] * own_mass))
    copies[1].start()
    for copy in copies:
        copy.wait()


def local(embeddings, prototypes, partner):
    n_batch, n_proto = lax.axis_size("batch"), lax.axis_size("proto")
    tiles = n_proto // 2
    rows, features = embeddings.shape
    own_protos = prototypes.shape[0]
    clips, protos = float(rows * n_batch * n_proto), float(own_protos * n_batch * n_proto)
    here, n_here = tiles * LANES, 2 * own_protos
    where = lax.axis_index("proto")
    side = int(tiles**0.5)
    crossed = [tile % side * side + tile // side for tile in range(tiles)]
    same_core = [[2 * chip for chip in crossed], [2 * chip + 1 for chip in range(tiles)]]
    rows_x = [[[2 * (side * y + x) + c for x in range(side)] for y in range(side)] for c in range(2)]
    rows_y = [[[2 * (side * y + x) + c for y in range(side)] for x in range(side)] for c in range(2)]
    cores = [(i, i ^ 1) for i in range(n_proto)]
    smem = pl.BlockSpec(memory_space=pltpu.SMEM)
    vmem = pl.BlockSpec(memory_space=pltpu.VMEM)

    def swap(values):
        return lax.ppermute(values, "proto", cores)

    def over_chips(blocks):
        return lax.all_to_all(blocks, "proto", 0, 0, tiled=True, axis_index_groups=same_core)

    def over_ring(blocks, groups):
        return lax.all_to_all(blocks, "proto", 0, 0, tiled=True, axis_index_groups=groups)

    def over_layers(lines):
        blocks = lax.all_to_all(lines.reshape(n_batch, 1, -1), "batch", 0, 0, tiled=True)
        return blocks.reshape(lines.shape)

    chip, core = where >> 1, where & 1
    tile = jnp.where(core > 0, chip, chip % side * side + chip // side)
    spot = jnp.stack([tile, lax.axis_index("batch"), core])
    partner = partner.reshape(-1, LANES)
    raw = jnp.concatenate([embeddings, partner.astype(jnp.float32)], axis=0)
    sent = call(functools.partial(send_body, n_proto, rows), f32(n_batch * raw.shape[0], LANES))(raw)
    sent, held, spot = lax.optimization_barrier((sent, prototypes, spot))
    column = over_layers(sent)
    own_units = call(units_body, f32(own_protos, features))(held)
    unit_protos = jnp.concatenate([own_units, swap(own_units)], axis=0)
    column, unit_protos = lax.optimization_barrier((column, unit_protos))
    blocks, places = call(
        column_body,
        (f32(tiles, LANES, features), jax.ShapeDtypeStruct((n_batch, partner.shape[0], LANES), jnp.int32)),
        in_specs=[smem, vmem],
    )(spot, column)
    own_clips = over_chips(blocks).reshape(here, features)

    e, totals, bundle = call(
        scores_body, (f32(n_here, here), f32(tiles, LANES), f32(n_here + here, features))
    )(unit_protos, own_clips)
    size = side * 2 * features + tiles
    pulls, table = call(functools.partial(pulls_body, side), (f32(side * size, LANES), f32(2 * here, features)))(
        unit_protos, e, own_clips
    )
    received, pulls, table = lax.optimization_barrier((swap(bundle), pulls, table))
    blocks = call(functools.partial(rows_first_body, protos), f32(tiles, tiles + 8, LANES))(e, bundle, received, totals)
    lines = call(spread_first_body, f32(n_batch * (tiles + 1), LANES))(over_chips(blocks))
    part, own_total = call(functools.partial(cols_first_body, clips), (f32(n_here, LANES), f32(8, LANES)))(
        e, over_layers(lines)
    )

    mates = pltpu.VMEM((2, PAIR, features), jnp.float32)
    part, late = lax.optimization_barrier((part, places.reshape(-1)))
    first_e, table = call(
        mates_first_body,
        (f32(n_here, here // 2), f32(2 * here, features)),
        in_specs=[smem, smem, vmem, vmem, vmem],
        scratch_shapes=[mates],
        input_output_aliases={4: 1},
    )(late, spot, unit_protos, received, table)
    other, first_e = lax.optimization_barrier((swap(part), first_e))
    blocks = call(functools.partial(rows_second_body, protos), f32(tiles, tiles + 8, LANES))(e, part, other, own_total)
    lines, totals = call(spread_second_body, (f32(n_batch * tiles, LANES), f32(tiles, LANES)))(over_chips(blocks))
    part = call(functools.partial(cols_second_body, clips), f32(n_here, LANES))(e, over_layers(lines))
    part, late = lax.optimization_barrier((part, late))
    second_e = call(
        mates_second_body, f32(n_here, here // 2), in_specs=[smem, smem, vmem, vmem], scratch_shapes=[mates]
    )(late, spot, unit_protos, table)
    other, second_e = lax.optimization_barrier((swap(part), second_e))
    lines, scale = call(
        functools.partial(mates_rows_body, protos, side),
        (f32(side * size, LANES), f32(n_here, LANES)),
        input_output_aliases={5: 0},
    )(first_e, second_e, part, other, unit_protos, pulls)
    blocks = over_ring(lines.reshape(side, size, LANES), rows_x[0] + rows_y[1])
    blocks = call(cross_body, f32(side, 2 * features + tiles, LANES))(blocks)
    blocks = over_ring(blocks, rows_y[0] + rows_x[1])
    lines = call(turn_body, f32(n_batch * (2 * rows + tiles), LANES))(blocks)
    other_grads, sums, inverse = call(
        other_grads_body, (f32(own_protos, features), f32(2 * rows, features), f32(2 * tiles, LANES))
    )(e, first_e, second_e, scale, totals, over_layers(lines), own_clips)
    own_grads = call(own_grads_body, f32(own_protos, features))(e, first_e, second_e, scale, inverse, own_clips)
    return call(
        finish_body, (f32(rows, features), f32(own_protos, features)), in_specs=[smem] + [vmem] * 6,
        out_specs=[pl.BlockSpec(memory_space=pl.ANY)] * 2,
        scratch_shapes=[
            pltpu.VMEM((rows, features), jnp.float32),
            pltpu.VMEM((own_protos, features), jnp.float32),
            pltpu.SemaphoreType.DMA((2,)),
        ],
    )(spot, inverse, sums, embeddings, prototypes, own_grads, swap(other_grads))


def solution(mesh):
    in_specs = (P(("batch", "proto"), None), P(("batch", "proto"), None), P("batch"))
    out_specs = (P(("batch", "proto"), None), P(("batch", "proto"), None))
    return jax.shard_map(local, mesh=mesh, in_specs=in_specs, out_specs=out_specs, check_vma=False)
```

```python
import functools

import jax
import jax.numpy as jnp
from jax import lax
from jax.experimental import pallas as pl
from jax.experimental.pallas import tpu as pltpu
from jax.sharding import PartitionSpec as P

LANES = 128
PAIR = 2 * LANES
CHUNK = 64
VMEM_BYTES = 24 * 1024 * 1024


def inverse_norms(values):
    return 1.0 / jnp.sqrt(jnp.sum(values * values, axis=1, keepdims=True) + 1e-06)


def finish_rows(values, grads):
    inverse = inverse_norms(values)
    units = values * inverse
    return inverse * (grads - units * jnp.sum(units * grads, axis=1, keepdims=True))


def split(values):
    high = values.astype(jnp.bfloat16)
    low = (values - high.astype(jnp.float32)).astype(jnp.bfloat16)
    return high, low


def dot(left, right):
    return jnp.dot(left, right, preferred_element_type=jnp.float32)


def dot_rows(left, right):
    return lax.dot_general(left, right, (((1,), (1,)), ((), ())), preferred_element_type=jnp.float32)


def call(body, out_shape, **kwargs):
    return pl.pallas_call(
        body, out_shape=out_shape, compiler_params=pltpu.CompilerParams(vmem_limit_bytes=VMEM_BYTES), **kwargs
    )


def f32(*shape):
    return jax.ShapeDtypeStruct(shape, jnp.float32)


def exponents(proto_pair, clips):
    high, low = split(clips)
    scores = dot_rows(proto_pair, jnp.concatenate([high, high], axis=1))
    scores = scores + dot_rows(proto_pair, jnp.concatenate([low, low], axis=1))
    return jnp.exp(scores * 10.0)


def scores_body(protos_ref, clips_ref, e_ref, total_ref, bundle_ref):
    n_here = protos_ref.shape[0]
    pair = jnp.concatenate(split(protos_ref[...]), axis=1)
    for block in range(clips_ref.shape[0] // PAIR):
        cols = slice(block * PAIR, (block + 1) * PAIR)
        clips = clips_ref[cols, :]
        bundle_ref[n_here + block * PAIR : n_here + (block + 1) * PAIR] = clips
        e = exponents(pair, clips)
        e_ref[:, cols] = e
        kernel = e * e
        both = kernel[:, :LANES] + kernel[:, LANES:]
        bundle_ref[:n_here] = both if block == 0 else bundle_ref[:n_here] + both
        totals = jnp.sum(e, axis=0, keepdims=True)
        for half in range(2):
            total_ref[2 * block + half : 2 * block + half + 1, :] = totals[:, half * LANES : (half + 1) * LANES]


def turned_protos(protos_ref):
    high, low = split(protos_ref[...].T)
    return jnp.concatenate([high, low], axis=0)


def times_protos(turned, weights):
    high, low = split(weights)
    both = dot(turned, high)
    return both[:LANES] + both[LANES:] + dot(turned[:LANES], low)


def ring_start(tile, side, size):
    return tile // side * size + tile % side * 2 * LANES


def pulls_body(side, protos_ref, e_ref, out_ref):
    turned = turned_protos(protos_ref)
    size = out_ref.shape[0] // side
    for block in range(e_ref.shape[1] // PAIR):
        x = times_protos(turned, e_ref[:, block * PAIR : (block + 1) * PAIR])
        for half in range(2):
            start = ring_start(2 * block + half, side, size)
            out_ref[start : start + LANES] = x[:, half * LANES : (half + 1) * LANES]


def mates_of(part, index_ref, spot_ref, protos_ref, table_ref, e_ref, mate_ref):
    pair = jnp.concatenate(split(protos_ref[...]), axis=1)
    blocks = e_ref.shape[1] // PAIR
    tiles = 4 * blocks
    core, side = spot_ref[2], int(tiles**0.5)
    for block in range(blocks):
        slot = block % 2
        for half in range(2):
            tile = 2 * (part * blocks + block) + half
            crossed = tile % side * side + tile // side
            first = crossed * 16 + core * ((tile - crossed) * 16 + 8)
            for z in range(LANES // 8):
                start = first + z * tiles * 16
                for r in range(8):
                    row = half * LANES + z * 8 + r
                    mate_ref[slot, row : row + 1, :] = table_ref[pl.ds(index_ref[start + r], 1), :]
        e_ref[:, block * PAIR : (block + 1) * PAIR] = exponents(pair, mate_ref[slot])


def mates_first_body(index_ref, spot_ref, protos_ref, own_ref, other_ref, e_ref, table_ref, mate_ref):
    rows = own_ref.shape[0]
    table_ref[:rows] = own_ref[...]
    table_ref[rows:] = other_ref[protos_ref.shape[0] :]
    mates_of(0, index_ref, spot_ref, protos_ref, table_ref, e_ref, mate_ref)


def mates_second_body(index_ref, spot_ref, protos_ref, table_ref, e_ref, mate_ref):
    mates_of(1, index_ref, spot_ref, protos_ref, table_ref, e_ref, mate_ref)


def column_scale(own_ref, other_ref, rows, protos):
    half = rows // 2
    part = jnp.concatenate([own_ref[:half] + other_ref[half:rows], own_ref[half:rows] + other_ref[:half]], axis=0)
    scale = 1.0 / (protos * jnp.sum(part, axis=1, keepdims=True))
    return jnp.broadcast_to(scale, (rows, LANES))


def row_mass(e_ref, scale, tile):
    e = e_ref[:, tile * LANES : (tile + 1) * LANES]
    return jnp.sum(e * e * scale, axis=0, keepdims=True)


def units_body(in_ref, out_ref):
    values = in_ref[...]
    out_ref[...] = values * inverse_norms(values)


def send_body(n_proto, rows, in_ref, out_ref):
    values = in_ref[:rows]
    partner = in_ref[rows:].astype(jnp.int32)
    line = partner & (rows - 1)
    slot = (partner // rows) & (n_proto - 1)
    side = int((n_proto // 2) ** 0.5)
    chip, core = slot >> 1, slot & 1
    tile = jnp.where(core > 0, chip, (chip & (side - 1)) * side + chip // side)
    place = core * (n_proto // 2) + tile
    place = place * LANES + partner // (rows * n_proto) * rows + line
    block = jnp.concatenate([values * inverse_norms(values), place.astype(jnp.float32)], axis=0)
    for layer in range(out_ref.shape[0] // block.shape[0]):
        out_ref[layer * block.shape[0] : (layer + 1) * block.shape[0]] = block


def column_body(spot_ref, in_ref, out_ref, places_ref):
    per_layer = places_ref.shape[1]
    size = 8 + per_layer
    places = []
    for layer in range(places_ref.shape[0]):
        units = in_ref[layer * size : layer * size + 8]
        places.append(in_ref[layer * size + 8 : (layer + 1) * size][None])
        for block in range(out_ref.shape[0]):
            out_ref[block, layer * 8 : layer * 8 + 8] = units
    here = out_ref.shape[0] * LANES
    places = jnp.concatenate(places, axis=0).astype(jnp.int32)
    moved = jnp.where(places >= here, places - here, places + here)
    places_ref[...] = jnp.where(spot_ref[2] > 0, moved, places)


def masses_of(e_ref, scale):
    tiles = e_ref.shape[1] // LANES
    return jnp.concatenate([row_mass(e_ref, scale, tile) for tile in range(tiles)], axis=0)


def rows_first_body(protos, e_ref, own_ref, other_ref, totals_ref, out_ref):
    tiles = e_ref.shape[1] // LANES
    scale = column_scale(own_ref, other_ref, e_ref.shape[0], protos)
    masses = masses_of(e_ref, scale)
    for block in range(tiles):
        out_ref[block, :tiles] = masses
        out_ref[block, tiles:] = jnp.broadcast_to(totals_ref[block : block + 1, :], (8, LANES))


def spread_first_body(in_ref, out_ref):
    tiles = in_ref.shape[0]
    total = jnp.sum(in_ref[...], axis=0)
    size = tiles + 1
    for layer in range(out_ref.shape[0] // size):
        out_ref[layer * size : (layer + 1) * size] = total[:size]


def weigh_columns(e_ref, scale, part_ref):
    tiles = e_ref.shape[1] // LANES
    for start in range(0, e_ref.shape[0], CHUNK):
        rows = slice(start, start + CHUNK)
        total = None
        for tile in range(tiles):
            e = e_ref[rows, tile * LANES : (tile + 1) * LANES]
            term = e * e * scale[tile : tile + 1, :]
            total = term if total is None else total + term
        part_ref[rows, :] = total


def cols_first_body(clips, e_ref, in_ref, part_ref, own_total_ref):
    tiles = e_ref.shape[1] // LANES
    size = tiles + 1
    total = in_ref[:size]
    for layer in range(1, in_ref.shape[0] // size):
        total = total + in_ref[layer * size : (layer + 1) * size]
    own_total_ref[...] = jnp.broadcast_to(total[tiles:], (8, LANES))
    weigh_columns(e_ref, 1.0 / (clips * total[:tiles]), part_ref)


def rows_second_body(protos, e_ref, own_ref, other_ref, own_total_ref, out_ref):
    tiles = e_ref.shape[1] // LANES
    masses = masses_of(e_ref, column_scale(own_ref, other_ref, e_ref.shape[0], protos))
    for block in range(tiles):
        out_ref[block, :tiles] = masses
        out_ref[block, tiles:] = own_total_ref[...]


def spread_second_body(in_ref, out_ref, totals_ref):
    tiles = in_ref.shape[0]
    masses = jnp.sum(in_ref[:, :tiles, :], axis=0)
    for layer in range(out_ref.shape[0] // tiles):
        out_ref[layer * tiles : (layer + 1) * tiles] = masses
    for block in range(tiles):
        totals_ref[block : block + 1, :] = in_ref[block, tiles : tiles + 1, :]


def summed_lines(in_ref, size):
    total = in_ref[:size]
    for layer in range(1, in_ref.shape[0] // size):
        total = total + in_ref[layer * size : (layer + 1) * size]
    return total


def cols_second_body(clips, e_ref, in_ref, part_ref):
    weigh_columns(e_ref, 1.0 / (clips * summed_lines(in_ref, e_ref.shape[1] // LANES)), part_ref)


def mates_rows_body(protos, side, first_ref, second_ref, own_ref, other_ref, protos_ref, _, out_ref, scale_ref):
    size = out_ref.shape[0] // side
    pair = 2 * LANES
    scale = column_scale(own_ref, other_ref, protos_ref.shape[0], protos)
    scale_ref[...] = scale
    wide = jnp.concatenate([scale, scale], axis=1)
    turned = turned_protos(protos_ref)
    masses = []
    blocks = first_ref.shape[1] // PAIR
    for block in range(2 * blocks):
        mate_e_ref = first_ref if block < blocks else second_ref
        start = block % blocks * PAIR
        e = mate_e_ref[:, start : start + PAIR]
        kernel = e * e * wide
        mass = jnp.sum(kernel, axis=0, keepdims=True)
        y = times_protos(turned, kernel)
        for half in range(2):
            lanes = slice(half * LANES, (half + 1) * LANES)
            masses.append(mass[:, lanes])
            start = ring_start(2 * block + half, side, size) + LANES
            out_ref[start : start + LANES] = y[:, lanes]
    masses = jnp.concatenate(masses, axis=0)
    for block in range(side):
        out_ref[block * size + side * pair : (block + 1) * size] = masses


def cross_body(in_ref, out_ref):
    side = out_ref.shape[0]
    pair = 2 * LANES
    total = jnp.sum(in_ref[...], axis=0)
    for block in range(side):
        out_ref[block, :pair] = total[block * pair : (block + 1) * pair]
        out_ref[block, pair:] = total[side * pair :]


def turn_body(in_ref, out_ref):
    total = jnp.sum(in_ref[...], axis=0)
    x, y, masses = total[:LANES].T, total[LANES : 2 * LANES].T, total[2 * LANES :]
    size = 16 + masses.shape[0]
    for layer in range(out_ref.shape[0] // size):
        base = layer * size
        out_ref[base : base + 8] = x[layer * 8 : layer * 8 + 8]
        out_ref[base + 8 : base + 16] = y[layer * 8 : layer * 8 + 8]
        out_ref[base + 16 : base + size] = masses


def proto_grads(rows, e_ref, first_ref, second_ref, scale_ref, shares, masses, clips_ref):
    scale = scale_ref[rows, :]
    blocks = first_ref.shape[1] // PAIR
    acc = None
    for block in range(2 * blocks):
        mate_e_ref = first_ref if block < blocks else second_ref
        pieces = []
        for half in range(2):
            tile = 2 * block + half
            mate = mate_e_ref[rows, (block % blocks * 2 + half) * LANES : (block % blocks * 2 + half + 1) * LANES]
            e = e_ref[rows, tile * LANES : (tile + 1) * LANES]
            pieces.append(e * shares[tile : tile + 1, :] - mate * mate * scale * masses[tile : tile + 1, :])
        high, low = split(jnp.concatenate(pieces, axis=1))
        clip_high, clip_low = split(clips_ref[block * PAIR : (block + 1) * PAIR, :])
        term = dot(high, jnp.concatenate([clip_high, clip_low], axis=1))
        term = term[:, :LANES] + term[:, LANES:] + dot(low, clip_high)
        acc = term if acc is None else acc + term
    return acc * 10.0


def other_grads_body(e_ref, first_ref, second_ref, scale_ref, totals_ref, in_ref, clips_ref, out_ref, sums_ref, inverse_ref):
    n_rows = out_ref.shape[0]
    tiles = totals_ref.shape[0]
    total = summed_lines(in_ref, 16 + tiles)
    sums_ref[...] = total[:16]
    masses = 1.0 / total[16:]
    shares = 1.0 / totals_ref[...]
    inverse_ref[:tiles] = masses
    inverse_ref[tiles:] = shares
    rows = slice(n_rows, 2 * n_rows)
    out_ref[...] = proto_grads(rows, e_ref, first_ref, second_ref, scale_ref, shares, masses, clips_ref)


def own_values(ref, row, layer):
    values = jnp.broadcast_to(ref[pl.ds(row, 1), :], (8, LANES))
    lane = lax.broadcasted_iota(jnp.int32, (8, LANES), 1)
    line = lax.broadcasted_iota(jnp.int32, (8, LANES), 0)
    return jnp.sum(jnp.where(lane == layer * 8 + line, values, 0.0), axis=1, keepdims=True)


def own_grads_body(e_ref, first_ref, second_ref, scale_ref, inverse_ref, clips_ref, out_ref):
    tiles = inverse_ref.shape[0] // 2
    rows = slice(0, out_ref.shape[0])
    out_ref[...] = proto_grads(
        rows, e_ref, first_ref, second_ref, scale_ref, inverse_ref[tiles:], inverse_ref[:tiles], clips_ref
    )


def finish_body(spot_ref, inverse_ref, sums_ref, embeddings_ref, protos_ref, own_ref, other_ref, clip_ref, proto_ref):
    tiles = inverse_ref.shape[0] // 2
    own_mass = own_values(inverse_ref, spot_ref[0], spot_ref[1])
    own_share = own_values(inverse_ref, spot_ref[0] + tiles, spot_ref[1])
    clip_ref[...] = finish_rows(embeddings_ref[...], 10.0 * (sums_ref[:8] * own_share - sums_ref[8:] * own_mass))
    proto_ref[...] = finish_rows(protos_ref[...], own_ref[...] + other_ref[...])


def local(embeddings, prototypes, partner):
    n_batch, n_proto = lax.axis_size("batch"), lax.axis_size("proto")
    tiles = n_proto // 2
    rows, features = embeddings.shape
    own_protos = prototypes.shape[0]
    clips, protos = float(rows * n_batch * n_proto), float(own_protos * n_batch * n_proto)
    here, n_here = tiles * LANES, 2 * own_protos
    where = lax.axis_index("proto")
    side = int(tiles**0.5)
    crossed = [tile % side * side + tile // side for tile in range(tiles)]
    same_core = [[2 * chip for chip in crossed], [2 * chip + 1 for chip in range(tiles)]]
    rows_x = [[[2 * (side * y + x) + c for x in range(side)] for y in range(side)] for c in range(2)]
    rows_y = [[[2 * (side * y + x) + c for y in range(side)] for x in range(side)] for c in range(2)]
    cores = [(i, i ^ 1) for i in range(n_proto)]
    smem = pl.BlockSpec(memory_space=pltpu.SMEM)
    vmem = pl.BlockSpec(memory_space=pltpu.VMEM)

    def swap(values):
        return lax.ppermute(values, "proto", cores)

    def over_chips(blocks):
        return lax.all_to_all(blocks, "proto", 0, 0, tiled=True, axis_index_groups=same_core)

    def over_ring(blocks, groups):
        return lax.all_to_all(blocks, "proto", 0, 0, tiled=True, axis_index_groups=groups)

    def over_layers(lines):
        blocks = lax.all_to_all(lines.reshape(n_batch, 1, -1), "batch", 0, 0, tiled=True)
        return blocks.reshape(lines.shape)

    chip, core = where >> 1, where & 1
    tile = jnp.where(core > 0, chip, chip % side * side + chip // side)
    spot = jnp.stack([tile, lax.axis_index("batch"), core])
    partner = partner.reshape(-1, LANES)
    n_values, n_mates = embeddings.size, partner.size
    values = jnp.pad(embeddings.reshape(-1), (0, n_mates))
    mates = jnp.pad(partner.reshape(-1), (n_values, 0)).astype(jnp.float32)
    raw = jnp.where(jnp.arange(n_values + n_mates) < n_values, values, mates).reshape(-1, LANES)
    sent = call(functools.partial(send_body, n_proto, rows), f32(n_batch * raw.shape[0], LANES))(raw)
    sent, held, spot = lax.optimization_barrier((sent, prototypes, spot))
    column = over_layers(sent)
    own_units = call(units_body, f32(own_protos, features))(held)
    unit_protos = jnp.concatenate([own_units, swap(own_units)], axis=0)
    column, unit_protos = lax.optimization_barrier((column, unit_protos))
    blocks, places = call(
        column_body,
        (f32(tiles, LANES, features), jax.ShapeDtypeStruct((n_batch, partner.shape[0], LANES), jnp.int32)),
        in_specs=[smem, vmem],
    )(spot, column)
    own_clips = over_chips(blocks).reshape(here, features)

    e, totals, bundle = call(
        scores_body, (f32(n_here, here), f32(tiles, LANES), f32(n_here + here, features))
    )(unit_protos, own_clips)
    size = side * 2 * features + tiles
    pulls = call(functools.partial(pulls_body, side), f32(side * size, LANES))(unit_protos, e)
    received, pulls = lax.optimization_barrier((swap(bundle), pulls))
    blocks = call(functools.partial(rows_first_body, protos), f32(tiles, tiles + 8, LANES))(e, bundle, received, totals)
    lines = call(spread_first_body, f32(n_batch * (tiles + 1), LANES))(over_chips(blocks))
    part, own_total = call(functools.partial(cols_first_body, clips), (f32(n_here, LANES), f32(8, LANES)))(
        e, over_layers(lines)
    )

    mates = pltpu.VMEM((2, PAIR, features), jnp.float32)
    part, late = lax.optimization_barrier((part, places.reshape(-1)))
    first_e, table = call(
        mates_first_body,
        (f32(n_here, here // 2), f32(2 * here, features)),
        in_specs=[smem, smem, vmem, vmem, vmem],
        scratch_shapes=[mates],
    )(late, spot, unit_protos, own_clips, received)
    other, first_e = lax.optimization_barrier((swap(part), first_e))
    blocks = call(functools.partial(rows_second_body, protos), f32(tiles, tiles + 8, LANES))(e, part, other, own_total)
    lines, totals = call(spread_second_body, (f32(n_batch * tiles, LANES), f32(tiles, LANES)))(over_chips(blocks))
    part = call(functools.partial(cols_second_body, clips), f32(n_here, LANES))(e, over_layers(lines))
    part, late = lax.optimization_barrier((part, late))
    second_e = call(
        mates_second_body, f32(n_here, here // 2), in_specs=[smem, smem, vmem, vmem], scratch_shapes=[mates]
    )(late, spot, unit_protos, table)
    other, second_e = lax.optimization_barrier((swap(part), second_e))
    lines, scale = call(
        functools.partial(mates_rows_body, protos, side),
        (f32(side * size, LANES), f32(n_here, LANES)),
        input_output_aliases={5: 0},
    )(first_e, second_e, part, other, unit_protos, pulls)
    blocks = over_ring(lines.reshape(side, size, LANES), rows_x[0] + rows_y[1])
    blocks = call(cross_body, f32(side, 2 * features + tiles, LANES))(blocks)
    blocks = over_ring(blocks, rows_y[0] + rows_x[1])
    lines = call(turn_body, f32(n_batch * (2 * rows + tiles), LANES))(blocks)
    other_grads, sums, inverse = call(
        other_grads_body, (f32(own_protos, features), f32(2 * rows, features), f32(2 * tiles, LANES))
    )(e, first_e, second_e, scale, totals, over_layers(lines), own_clips)
    own_grads = call(own_grads_body, f32(own_protos, features))(e, first_e, second_e, scale, inverse, own_clips)
    return call(
        finish_body, (f32(rows, features), f32(own_protos, features)), in_specs=[smem] + [vmem] * 6
    )(spot, inverse, sums, embeddings, prototypes, own_grads, swap(other_grads))


def solution(mesh):
    in_specs = (P(("batch", "proto"), None), P(("batch", "proto"), None), P("batch"))
    out_specs = (P(("batch", "proto"), None), P(("batch", "proto"), None))
    return jax.shard_map(local, mesh=mesh, in_specs=in_specs, out_specs=out_specs, check_vma=False)
```

```python
import functools

import jax
import jax.numpy as jnp
from jax import lax
from jax.experimental import pallas as pl
from jax.experimental.pallas import tpu as pltpu
from jax.sharding import PartitionSpec as P

LANES = 128
PAIR = 2 * LANES
CHUNK = 64
VMEM_BYTES = 24 * 1024 * 1024


def inverse_norms(values):
    return 1.0 / jnp.sqrt(jnp.sum(values * values, axis=1, keepdims=True) + 1e-06)


def finish_rows(values, grads):
    inverse = inverse_norms(values)
    units = values * inverse
    return inverse * (grads - units * jnp.sum(units * grads, axis=1, keepdims=True))


def split(values):
    high = values.astype(jnp.bfloat16)
    low = (values - high.astype(jnp.float32)).astype(jnp.bfloat16)
    return high, low


def dot(left, right):
    return jnp.dot(left, right, preferred_element_type=jnp.float32)


def dot_rows(left, right):
    return lax.dot_general(left, right, (((1,), (1,)), ((), ())), preferred_element_type=jnp.float32)


def call(body, out_shape, **kwargs):
    return pl.pallas_call(
        body, out_shape=out_shape, compiler_params=pltpu.CompilerParams(vmem_limit_bytes=VMEM_BYTES), **kwargs
    )


def f32(*shape):
    return jax.ShapeDtypeStruct(shape, jnp.float32)


def exponents(proto_pair, clips):
    high, low = split(clips)
    scores = dot_rows(proto_pair, jnp.concatenate([high, high], axis=1))
    scores = scores + dot_rows(proto_pair, jnp.concatenate([low, low], axis=1))
    return jnp.exp(scores * 10.0)


def scores_body(protos_ref, clips_ref, e_ref, total_ref, bundle_ref):
    n_here = protos_ref.shape[0]
    pair = jnp.concatenate(split(protos_ref[...]), axis=1)
    for block in range(clips_ref.shape[0] // PAIR):
        cols = slice(block * PAIR, (block + 1) * PAIR)
        clips = clips_ref[cols, :]
        bundle_ref[n_here + block * PAIR : n_here + (block + 1) * PAIR] = clips
        e = exponents(pair, clips)
        e_ref[:, cols] = e
        kernel = e * e
        both = kernel[:, :LANES] + kernel[:, LANES:]
        bundle_ref[:n_here] = both if block == 0 else bundle_ref[:n_here] + both
        totals = jnp.sum(e, axis=0, keepdims=True)
        for half in range(2):
            total_ref[2 * block + half : 2 * block + half + 1, :] = totals[:, half * LANES : (half + 1) * LANES]


def turned_protos(protos_ref):
    high, low = split(protos_ref[...].T)
    return jnp.concatenate([high, low], axis=0)


def times_protos(turned, weights):
    high, low = split(weights)
    both = dot(turned, high)
    return both[:LANES] + both[LANES:] + dot(turned[:LANES], low)


def ring_start(tile, side, size):
    return tile // side * size + tile % side * 2 * LANES


def pulls_body(side, protos_ref, e_ref, out_ref):
    turned = turned_protos(protos_ref)
    size = out_ref.shape[0] // side
    for block in range(e_ref.shape[1] // PAIR):
        x = times_protos(turned, e_ref[:, block * PAIR : (block + 1) * PAIR])
        for half in range(2):
            start = ring_start(2 * block + half, side, size)
            out_ref[start : start + LANES] = x[:, half * LANES : (half + 1) * LANES]


def mates_of(part, index_ref, spot_ref, protos_ref, table_ref, e_ref, mate_ref):
    pair = jnp.concatenate(split(protos_ref[...]), axis=1)
    blocks = e_ref.shape[1] // PAIR
    tiles = 4 * blocks
    core, side = spot_ref[2], int(tiles**0.5)
    for block in range(blocks):
        slot = block % 2
        for half in range(2):
            tile = 2 * (part * blocks + block) + half
            crossed = tile % side * side + tile // side
            first = crossed * 16 + core * ((tile - crossed) * 16 + 8)
            for z in range(LANES // 8):
                start = first + z * tiles * 16
                for r in range(8):
                    row = half * LANES + z * 8 + r
                    mate_ref[slot, row : row + 1, :] = table_ref[pl.ds(index_ref[start + r], 1), :]
        e_ref[:, block * PAIR : (block + 1) * PAIR] = exponents(pair, mate_ref[slot])


def mates_first_body(index_ref, spot_ref, protos_ref, own_ref, other_ref, e_ref, table_ref, mate_ref):
    rows = own_ref.shape[0]
    table_ref[:rows] = own_ref[...]
    table_ref[rows:] = other_ref[protos_ref.shape[0] :]
    mates_of(0, index_ref, spot_ref, protos_ref, table_ref, e_ref, mate_ref)


def mates_second_body(index_ref, spot_ref, protos_ref, table_ref, e_ref, mate_ref):
    mates_of(1, index_ref, spot_ref, protos_ref, table_ref, e_ref, mate_ref)


def column_scale(own_ref, other_ref, rows, protos):
    half = rows // 2
    part = jnp.concatenate([own_ref[:half] + other_ref[half:rows], own_ref[half:rows] + other_ref[:half]], axis=0)
    scale = 1.0 / (protos * jnp.sum(part, axis=1, keepdims=True))
    return jnp.broadcast_to(scale, (rows, LANES))


def row_mass(e_ref, scale, tile):
    e = e_ref[:, tile * LANES : (tile + 1) * LANES]
    return jnp.sum(e * e * scale, axis=0, keepdims=True)


def units_body(in_ref, out_ref):
    values = in_ref[...]
    out_ref[...] = values * inverse_norms(values)


def send_body(n_proto, rows, in_ref, out_ref):
    values = in_ref[:rows]
    partner = in_ref[rows:].astype(jnp.int32)
    line = partner & (rows - 1)
    slot = (partner // rows) & (n_proto - 1)
    side = int((n_proto // 2) ** 0.5)
    chip, core = slot >> 1, slot & 1
    tile = jnp.where(core > 0, chip, (chip & (side - 1)) * side + chip // side)
    place = core * (n_proto // 2) + tile
    place = place * LANES + partner // (rows * n_proto) * rows + line
    block = jnp.concatenate([values * inverse_norms(values), place.astype(jnp.float32)], axis=0)
    for layer in range(out_ref.shape[0] // block.shape[0]):
        out_ref[layer * block.shape[0] : (layer + 1) * block.shape[0]] = block


def column_body(spot_ref, in_ref, out_ref, places_ref):
    per_layer = places_ref.shape[1]
    size = 8 + per_layer
    places = []
    for layer in range(places_ref.shape[0]):
        units = in_ref[layer * size : layer * size + 8]
        places.append(in_ref[layer * size + 8 : (layer + 1) * size][None])
        for block in range(out_ref.shape[0]):
            out_ref[block, layer * 8 : layer * 8 + 8] = units
    here = out_ref.shape[0] * LANES
    places = jnp.concatenate(places, axis=0).astype(jnp.int32)
    moved = jnp.where(places >= here, places - here, places + here)
    places_ref[...] = jnp.where(spot_ref[2] > 0, moved, places)


def masses_of(e_ref, scale):
    tiles = e_ref.shape[1] // LANES
    return jnp.concatenate([row_mass(e_ref, scale, tile) for tile in range(tiles)], axis=0)


def rows_first_body(protos, e_ref, own_ref, other_ref, totals_ref, out_ref):
    tiles = e_ref.shape[1] // LANES
    scale = column_scale(own_ref, other_ref, e_ref.shape[0], protos)
    masses = masses_of(e_ref, scale)
    for block in range(tiles):
        out_ref[block, :tiles] = masses
        out_ref[block, tiles:] = jnp.broadcast_to(totals_ref[block : block + 1, :], (8, LANES))


def spread_first_body(in_ref, out_ref):
    tiles = in_ref.shape[0]
    total = jnp.sum(in_ref[...], axis=0)
    size = tiles + 1
    for layer in range(out_ref.shape[0] // size):
        out_ref[layer * size : (layer + 1) * size] = total[:size]


def weigh_columns(e_ref, scale, part_ref):
    tiles = e_ref.shape[1] // LANES
    for start in range(0, e_ref.shape[0], CHUNK):
        rows = slice(start, start + CHUNK)
        total = None
        for tile in range(tiles):
            e = e_ref[rows, tile * LANES : (tile + 1) * LANES]
            term = e * e * scale[tile : tile + 1, :]
            total = term if total is None else total + term
        part_ref[rows, :] = total


def cols_first_body(clips, e_ref, in_ref, part_ref, own_total_ref):
    tiles = e_ref.shape[1] // LANES
    size = tiles + 1
    total = in_ref[:size]
    for layer in range(1, in_ref.shape[0] // size):
        total = total + in_ref[layer * size : (layer + 1) * size]
    own_total_ref[...] = jnp.broadcast_to(total[tiles:], (8, LANES))
    weigh_columns(e_ref, 1.0 / (clips * total[:tiles]), part_ref)


def rows_second_body(protos, e_ref, own_ref, other_ref, own_total_ref, out_ref):
    tiles = e_ref.shape[1] // LANES
    masses = masses_of(e_ref, column_scale(own_ref, other_ref, e_ref.shape[0], protos))
    for block in range(tiles):
        out_ref[block, :tiles] = masses
        out_ref[block, tiles:] = own_total_ref[...]


def spread_second_body(in_ref, out_ref, totals_ref):
    tiles = in_ref.shape[0]
    masses = jnp.sum(in_ref[:, :tiles, :], axis=0)
    for layer in range(out_ref.shape[0] // tiles):
        out_ref[layer * tiles : (layer + 1) * tiles] = masses
    for block in range(tiles):
        totals_ref[block : block + 1, :] = in_ref[block, tiles : tiles + 1, :]


def summed_lines(in_ref, size):
    total = in_ref[:size]
    for layer in range(1, in_ref.shape[0] // size):
        total = total + in_ref[layer * size : (layer + 1) * size]
    return total


def cols_second_body(clips, e_ref, in_ref, part_ref):
    weigh_columns(e_ref, 1.0 / (clips * summed_lines(in_ref, e_ref.shape[1] // LANES)), part_ref)


def mates_rows_body(protos, side, first_ref, second_ref, own_ref, other_ref, protos_ref, _, out_ref, scale_ref):
    size = out_ref.shape[0] // side
    pair = 2 * LANES
    scale = column_scale(own_ref, other_ref, protos_ref.shape[0], protos)
    scale_ref[...] = scale
    wide = jnp.concatenate([scale, scale], axis=1)
    turned = turned_protos(protos_ref)
    masses = []
    blocks = first_ref.shape[1] // PAIR
    for block in range(2 * blocks):
        mate_e_ref = first_ref if block < blocks else second_ref
        start = block % blocks * PAIR
        e = mate_e_ref[:, start : start + PAIR]
        kernel = e * e * wide
        mass = jnp.sum(kernel, axis=0, keepdims=True)
        y = times_protos(turned, kernel)
        for half in range(2):
            lanes = slice(half * LANES, (half + 1) * LANES)
            masses.append(mass[:, lanes])
            start = ring_start(2 * block + half, side, size) + LANES
            out_ref[start : start + LANES] = y[:, lanes]
    masses = jnp.concatenate(masses, axis=0)
    for block in range(side):
        out_ref[block * size + side * pair : (block + 1) * size] = masses


def cross_body(in_ref, out_ref):
    side = out_ref.shape[0]
    pair = 2 * LANES
    total = jnp.sum(in_ref[...], axis=0)
    for block in range(side):
        out_ref[block, :pair] = total[block * pair : (block + 1) * pair]
        out_ref[block, pair:] = total[side * pair :]


def turn_body(in_ref, out_ref):
    total = jnp.sum(in_ref[...], axis=0)
    x, y, masses = total[:LANES].T, total[LANES : 2 * LANES].T, total[2 * LANES :]
    size = 16 + masses.shape[0]
    for layer in range(out_ref.shape[0] // size):
        base = layer * size
        out_ref[base : base + 8] = x[layer * 8 : layer * 8 + 8]
        out_ref[base + 8 : base + 16] = y[layer * 8 : layer * 8 + 8]
        out_ref[base + 16 : base + size] = masses


def proto_grads(rows, e_ref, first_ref, second_ref, scale_ref, shares, masses, clips_ref):
    scale = scale_ref[rows, :]
    blocks = first_ref.shape[1] // PAIR
    acc = None
    for block in range(2 * blocks):
        mate_e_ref = first_ref if block < blocks else second_ref
        pieces = []
        for half in range(2):
            tile = 2 * block + half
            mate = mate_e_ref[rows, (block % blocks * 2 + half) * LANES : (block % blocks * 2 + half + 1) * LANES]
            e = e_ref[rows, tile * LANES : (tile + 1) * LANES]
            pieces.append(e * shares[tile : tile + 1, :] - mate * mate * scale * masses[tile : tile + 1, :])
        high, low = split(jnp.concatenate(pieces, axis=1))
        clip_high, clip_low = split(clips_ref[block * PAIR : (block + 1) * PAIR, :])
        term = dot(high, jnp.concatenate([clip_high, clip_low], axis=1))
        term = term[:, :LANES] + term[:, LANES:] + dot(low, clip_high)
        acc = term if acc is None else acc + term
    return acc * 10.0


def other_grads_body(e_ref, first_ref, second_ref, scale_ref, totals_ref, in_ref, clips_ref, out_ref, sums_ref, inverse_ref):
    n_rows = out_ref.shape[0]
    tiles = totals_ref.shape[0]
    total = summed_lines(in_ref, 16 + tiles)
    sums_ref[...] = total[:16]
    masses = 1.0 / total[16:]
    shares = 1.0 / totals_ref[...]
    inverse_ref[:tiles] = masses
    inverse_ref[tiles:] = shares
    rows = slice(n_rows, 2 * n_rows)
    out_ref[...] = proto_grads(rows, e_ref, first_ref, second_ref, scale_ref, shares, masses, clips_ref)


def own_values(ref, row, layer):
    values = jnp.broadcast_to(ref[pl.ds(row, 1), :], (8, LANES))
    lane = lax.broadcasted_iota(jnp.int32, (8, LANES), 1)
    line = lax.broadcasted_iota(jnp.int32, (8, LANES), 0)
    return jnp.sum(jnp.where(lane == layer * 8 + line, values, 0.0), axis=1, keepdims=True)


def own_grads_body(spot_ref, e_ref, first_ref, second_ref, scale_ref, inverse_ref, clips_ref, sums_ref, embeddings_ref,
                   out_ref, clip_ref):
    tiles = inverse_ref.shape[0] // 2
    own_mass = own_values(inverse_ref, spot_ref[0], spot_ref[1])
    own_share = own_values(inverse_ref, spot_ref[0] + tiles, spot_ref[1])
    clip_ref[...] = finish_rows(embeddings_ref[...], 10.0 * (sums_ref[:8] * own_share - sums_ref[8:] * own_mass))
    rows = slice(0, out_ref.shape[0])
    out_ref[...] = proto_grads(
        rows, e_ref, first_ref, second_ref, scale_ref, inverse_ref[tiles:], inverse_ref[:tiles], clips_ref
    )


def finish_body(held_ref, protos_ref, own_ref, other_ref, clip_ref, proto_ref):
    clip_ref[...] = held_ref[...]
    proto_ref[...] = finish_rows(protos_ref[...], own_ref[...] + other_ref[...])


def local(embeddings, prototypes, partner):
    n_batch, n_proto = lax.axis_size("batch"), lax.axis_size("proto")
    tiles = n_proto // 2
    rows, features = embeddings.shape
    own_protos = prototypes.shape[0]
    clips, protos = float(rows * n_batch * n_proto), float(own_protos * n_batch * n_proto)
    here, n_here = tiles * LANES, 2 * own_protos
    where = lax.axis_index("proto")
    side = int(tiles**0.5)
    crossed = [tile % side * side + tile // side for tile in range(tiles)]
    same_core = [[2 * chip for chip in crossed], [2 * chip + 1 for chip in range(tiles)]]
    rows_x = [[[2 * (side * y + x) + c for x in range(side)] for y in range(side)] for c in range(2)]
    rows_y = [[[2 * (side * y + x) + c for y in range(side)] for x in range(side)] for c in range(2)]
    cores = [(i, i ^ 1) for i in range(n_proto)]
    smem = pl.BlockSpec(memory_space=pltpu.SMEM)
    vmem = pl.BlockSpec(memory_space=pltpu.VMEM)

    def swap(values):
        return lax.ppermute(values, "proto", cores)

    def over_chips(blocks):
        return lax.all_to_all(blocks, "proto", 0, 0, tiled=True, axis_index_groups=same_core)

    def over_ring(blocks, groups):
        return lax.all_to_all(blocks, "proto", 0, 0, tiled=True, axis_index_groups=groups)

    def over_layers(lines):
        blocks = lax.all_to_all(lines.reshape(n_batch, 1, -1), "batch", 0, 0, tiled=True)
        return blocks.reshape(lines.shape)

    chip, core = where >> 1, where & 1
    tile = jnp.where(core > 0, chip, chip % side * side + chip // side)
    spot = jnp.stack([tile, lax.axis_index("batch"), core])
    partner = partner.reshape(-1, LANES)
    n_values, n_mates = embeddings.size, partner.size
    values = jnp.pad(embeddings.reshape(-1), (0, n_mates))
    mates = jnp.pad(partner.reshape(-1), (n_values, 0)).astype(jnp.float32)
    raw = jnp.where(jnp.arange(n_values + n_mates) < n_values, values, mates).reshape(-1, LANES)
    sent = call(functools.partial(send_body, n_proto, rows), f32(n_batch * raw.shape[0], LANES))(raw)
    sent, held, spot = lax.optimization_barrier((sent, prototypes, spot))
    column = over_layers(sent)
    own_units = call(units_body, f32(own_protos, features))(held)
    unit_protos = jnp.concatenate([own_units, swap(own_units)], axis=0)
    column, unit_protos = lax.optimization_barrier((column, unit_protos))
    blocks, places = call(
        column_body,
        (f32(tiles, LANES, features), jax.ShapeDtypeStruct((n_batch, partner.shape[0], LANES), jnp.int32)),
        in_specs=[smem, vmem],
    )(spot, column)
    own_clips = over_chips(blocks).reshape(here, features)

    e, totals, bundle = call(
        scores_body, (f32(n_here, here), f32(tiles, LANES), f32(n_here + here, features))
    )(unit_protos, own_clips)
    size = side * 2 * features + tiles
    pulls = call(functools.partial(pulls_body, side), f32(side * size, LANES))(unit_protos, e)
    received, pulls = lax.optimization_barrier((swap(bundle), pulls))
    blocks = call(functools.partial(rows_first_body, protos), f32(tiles, tiles + 8, LANES))(e, bundle, received, totals)
    lines = call(spread_first_body, f32(n_batch * (tiles + 1), LANES))(over_chips(blocks))
    part, own_total = call(functools.partial(cols_first_body, clips), (f32(n_here, LANES), f32(8, LANES)))(
        e, over_layers(lines)
    )

    mates = pltpu.VMEM((2, PAIR, features), jnp.float32)
    part, late = lax.optimization_barrier((part, places.reshape(-1)))
    first_e, table = call(
        mates_first_body,
        (f32(n_here, here // 2), f32(2 * here, features)),
        in_specs=[smem, smem, vmem, vmem, vmem],
        scratch_shapes=[mates],
    )(late, spot, unit_protos, own_clips, received)
    other, first_e = lax.optimization_barrier((swap(part), first_e))
    blocks = call(functools.partial(rows_second_body, protos), f32(tiles, tiles + 8, LANES))(e, part, other, own_total)
    lines, totals = call(spread_second_body, (f32(n_batch * tiles, LANES), f32(tiles, LANES)))(over_chips(blocks))
    part = call(functools.partial(cols_second_body, clips), f32(n_here, LANES))(e, over_layers(lines))
    part, late = lax.optimization_barrier((part, late))
    second_e = call(
        mates_second_body, f32(n_here, here // 2), in_specs=[smem, smem, vmem, vmem], scratch_shapes=[mates]
    )(late, spot, unit_protos, table)
    other, second_e = lax.optimization_barrier((swap(part), second_e))
    lines, scale = call(
        functools.partial(mates_rows_body, protos, side),
        (f32(side * size, LANES), f32(n_here, LANES)),
        input_output_aliases={5: 0},
    )(first_e, second_e, part, other, unit_protos, pulls)
    blocks = over_ring(lines.reshape(side, size, LANES), rows_x[0] + rows_y[1])
    blocks = call(cross_body, f32(side, 2 * features + tiles, LANES))(blocks)
    blocks = over_ring(blocks, rows_y[0] + rows_x[1])
    lines = call(turn_body, f32(n_batch * (2 * rows + tiles), LANES))(blocks)
    other_grads, sums, inverse = call(
        other_grads_body, (f32(own_protos, features), f32(2 * rows, features), f32(2 * tiles, LANES))
    )(e, first_e, second_e, scale, totals, over_layers(lines), own_clips)
    own_grads, held = call(
        own_grads_body, (f32(own_protos, features), f32(rows, features)), in_specs=[smem] + [vmem] * 8
    )(spot, e, first_e, second_e, scale, inverse, own_clips, sums, embeddings)
    return call(finish_body, (f32(rows, features), f32(own_protos, features)))(
        held, prototypes, own_grads, swap(other_grads)
    )


def solution(mesh):
    in_specs = (P(("batch", "proto"), None), P(("batch", "proto"), None), P("batch"))
    out_specs = (P(("batch", "proto"), None), P(("batch", "proto"), None))
    return jax.shard_map(local, mesh=mesh, in_specs=in_specs, out_specs=out_specs, check_vma=False)
```
